32 devices in a mesh: ctx: 16 (over z, x, core), head: 2 (over y).
Axes of the slice: x: 2, y: 2, z: 4, core: 2. Of those that a mesh axis runs over, the one named last changes fastest.
Arguments:
- query_rows: bfloat16 [3072, 8192], P('ctx', 'head'), may hold values from -6 to 6
- key_rows: bfloat16 [3072, 1024], P('ctx', 'head'), may hold values from -6 to 6
- value_rows: bfloat16 [3072, 1024], P('ctx', 'head'), may hold values from -6 to 6
- attn_output: bfloat16 [3072, 8192], P('ctx', 'head'), may hold values from -6 to 6
- log_norms: float32 [64, 3072], P('head', 'ctx'), may hold values from 3 to 5
- grad_output: bfloat16 [3072, 8192], P(('ctx', 'head')), may hold values from -2.390625 to 2.390625
- span_order: int32 [32], replicated, may hold values from 0 to 31, each once
Outputs:
- grad_query: bfloat16 [3072, 8192], P(('ctx', 'head'))
- grad_key: bfloat16 [3072, 1024], P('ctx', 'head')
- grad_value: bfloat16 [3072, 1024], P('ctx', 'head')
The draws below stay inside these ranges and needn't reach their ends.
Inputs may be any that keep to these rules, and one draw needn't show every extreme that they name: span_order is a permutation: each of the 32 spans of 96 positions is held by exactly one slot.
All inputs are finite; a program needn't handle non-finite values.
Results may differ from the reference program's by a relative error of at most 0.0051.
Values may be sent and summed in bfloat16 or wider, within the bound.
A program may use at most 192 MiB of HBM per device.

```python
import jax
import jax.numpy as jnp
from jax import lax

QH = 64
KVH = 8
HD = 128
TOK_DEV = 192
SPANS = 32
SEQ = 3072


def steps_of(stream_key, shape, cuts, smallest, high):
    gain = 1.0
    for position, blocks in cuts:
        heights = jax.random.uniform(jax.random.fold_in(jax.random.fold_in(stream_key, 6), position), (blocks,), jnp.float32, smallest / len(cuts), high / len(cuts))
        gain = gain * jnp.repeat(jnp.exp(heights), shape[position] // blocks).reshape((-1,) + (1,) * (len(shape) - 1 - position))
    return gain


def centred(own_key, shape, width, bound, pieces=(), kind=jnp.bfloat16):
    result = width * jax.random.normal(own_key, shape, jnp.float32)
    if pieces:
        result = result * steps_of(own_key, shape, pieces, -0.22, 0.18)
    return jnp.clip(result, -bound, bound).astype(kind)


def setup_inputs(seed: int = 0) -> dict:
    splits = jax.random.split(jax.random.key(seed), 8)
    return {
        "query_rows": centred(splits[0], (SEQ, QH * HD), 1.0, 6.0, ((0, 16), (1, 2))),
        "key_rows": centred(splits[1], (SEQ, KVH * HD), 1.0, 6.0, ((0, 16), (1, 2))),
        "value_rows": centred(splits[2], (SEQ, KVH * HD), 1.0, 6.0, ((0, 16), (1, 2))),
        "attn_output": centred(splits[3], (SEQ, QH * HD), 1.0, 6.0, ((0, 16), (1, 2))),
        "log_norms": jnp.clip(3.0 + 2.0 * jax.random.uniform(splits[4], (QH, SEQ), jnp.float32) ** steps_of(splits[4], (QH, SEQ), ((0, 2), (1, 16)), -0.2, 0.2), 3.0, 5.0),
        "grad_output": centred(splits[5], (SEQ, QH * HD), 0.3, 2.390625, ((0, 32),)),
        "span_order": jax.random.permutation(splits[6], SPANS).astype(jnp.int32),
    }


def reference(query_rows, key_rows, value_rows, attn_output, log_norms, grad_output, span_order):
    seq_len = query_rows.shape[0]
    groups = QH // KVH
    half_span = TOK_DEV // 2
    row_ids = jnp.arange(seq_len, dtype=jnp.int32)
    slot_ids = row_ids // half_span
    slot_match = slot_ids[:, None] == jnp.arange(SPANS, dtype=jnp.int32)[None, :]
    span_ids = jnp.sum(jnp.where(slot_match, span_order[None, :], 0), axis=1).astype(jnp.int32)
    positions = span_ids * half_span + row_ids % half_span
    query_heads = query_rows.reshape(seq_len, KVH, groups, HD)
    grad_heads = grad_output.reshape(seq_len, KVH, groups, HD)
    out_heads = attn_output.reshape(seq_len, KVH, groups, HD)
    row_delta = jnp.sum(grad_heads.astype(jnp.float32) * out_heads.astype(jnp.float32), axis=-1)
    lse_rows = log_norms.reshape(KVH, groups, seq_len).transpose(2, 0, 1)
    inv_root = HD ** -0.5
    blocks = seq_len // TOK_DEV

    def one_head(inputs):
        q_head, d_head, delta_head, lse_head, k_head, v_head = inputs
        key_float = k_head.astype(jnp.float32)
        value_float = v_head.astype(jnp.float32)

        def one_block(carry_state, block_id):
            dk_acc, dv_acc = carry_state
            row_start = (block_id * TOK_DEV).astype(jnp.int32)
            q_block = lax.dynamic_slice_in_dim(q_head, row_start, TOK_DEV, 0).astype(jnp.float32)
            d_block = lax.dynamic_slice_in_dim(d_head, row_start, TOK_DEV, 0).astype(jnp.float32)
            delta_block = lax.dynamic_slice_in_dim(delta_head, row_start, TOK_DEV, 0)
            lse_block = lax.dynamic_slice_in_dim(lse_head, row_start, TOK_DEV, 0)
            pos_block = lax.dynamic_slice_in_dim(positions, row_start, TOK_DEV, 0)
            scores = jnp.einsum("tgd,sd->tgs", q_block, key_float) * inv_root
            causal = pos_block[:, None, None] >= positions[None, None, :]
            prob_full = jnp.where(causal, jnp.exp(scores - lse_block[..., None]), 0.0)
            prob_low = lax.optimization_barrier(prob_full.astype(jnp.bfloat16)).astype(jnp.float32)
            dprobs = jnp.einsum("tgd,sd->tgs", d_block, value_float)
            dscores = (prob_full * (dprobs - delta_block[..., None])).astype(jnp.bfloat16)
            dscores = lax.optimization_barrier(dscores).astype(jnp.float32)
            dq_block = jnp.einsum("tgs,sd->tgd", dscores, key_float) * inv_root
            dk_acc = dk_acc + jnp.einsum("tgs,tgd->sd", dscores, q_block) * inv_root
            dv_acc = dv_acc + jnp.einsum("tgs,tgd->sd", prob_low, d_block)
            return (dk_acc, dv_acc), dq_block.astype(jnp.bfloat16)

        empty_acc = jnp.zeros((seq_len, HD), jnp.float32)
        (dk_acc, dv_acc), dq_parts = lax.scan(one_block, (empty_acc, empty_acc), jnp.arange(blocks, dtype=jnp.int32))
        return dq_parts.reshape(seq_len, groups, HD), dk_acc.astype(jnp.bfloat16), dv_acc.astype(jnp.bfloat16)

    dq_all, dk_all, dv_all = lax.map(one_head, (
        query_heads.transpose(1, 0, 2, 3), grad_heads.transpose(1, 0, 2, 3),
        row_delta.transpose(1, 0, 2), lse_rows.transpose(1, 0, 2),
        key_rows.reshape(seq_len, KVH, HD).transpose(1, 0, 2),
        value_rows.reshape(seq_len, KVH, HD).transpose(1, 0, 2)))
    grad_query = dq_all.transpose(1, 0, 2, 3).reshape(seq_len, QH * HD)
    grad_key = dk_all.transpose(1, 0, 2).reshape(seq_len, KVH * HD)
    grad_value = dv_all.transpose(1, 0, 2).reshape(seq_len, KVH * HD)
    return (grad_query, grad_key, grad_value)
```

```python
import functools
import math

import jax
import jax.numpy as jnp
from jax import lax
from jax.experimental import pallas as pl
from jax.experimental.pallas import tpu as pltpu
from jax.sharding import PartitionSpec as P

QH = 64
KVH = 8
HD = 128
GROUPS = QH // KVH
KEYS = 256
LOG2E = math.log2(math.e)


def attend_kernel(
    slot_of_ref, my_span_ref,
    q_ref, d_ref, k_ref, v_ref, lse_ref, delta_ref, base_ref,
    dq_ref, dk_ref, dv_ref,
    ks, kt, vs, qs, qt, ds_rows, dt, dqt, dk_acc, dv_acc,
):
    span = base_ref.shape[1] // GROUPS
    seq = k_ref.shape[0]
    slots = q_ref.shape[0] // span
    inv_root = HD ** -0.5

    def place(p, _):
        src = pl.ds(pl.multiple_of(slot_of_ref[p] * span, span), span)
        dst = pl.ds(pl.multiple_of(p * span, span), span)
        ks[dst, :] = k_ref[src, :]
        vs[dst, :] = v_ref[src, :]
        return 0

    lax.fori_loop(0, seq // span, place, 0)

    def turn(c, _):
        rows = pl.ds(pl.multiple_of(c * KEYS, KEYS), KEYS)
        kt[c] = ks[rows, :].T
        dk_acc[rows, :] = jnp.zeros((KEYS, HD), jnp.float32)
        dv_acc[rows, :] = jnp.zeros((KEYS, HD), jnp.float32)
        return 0

    lax.fori_loop(0, seq // KEYS, turn, 0)

    def one_slot(s, _):
        rows = pl.ds(pl.multiple_of(s * span, span), span)
        for g in range(GROUPS):
            part = slice(g * span, (g + 1) * span)
            cols = slice(g * HD, (g + 1) * HD)
            qs[part, :] = q_ref[rows, cols]
            ds_rows[part, :] = d_ref[rows, cols]
        qt[...] = qs[...].T
        dt[...] = ds_rows[...].T
        dqt[...] = jnp.zeros_like(dqt)
        my_span = my_span_ref[s]

        def block(c, masked):
            keys = pl.ds(pl.multiple_of(c * KEYS, KEYS), KEYS)
            scores = jnp.dot(ks[keys, :], qt[...], preferred_element_type=jnp.float32)
            prob = jnp.exp2(scores * (inv_root * LOG2E) - lse_ref[0, s])
            if masked:
                key_pos = c * KEYS + lax.broadcasted_iota(jnp.int32, prob.shape, 0)
                prob = jnp.where(my_span * span + base_ref[...] >= key_pos, prob, 0.0)
            dprob = jnp.dot(vs[keys, :], dt[...], preferred_element_type=jnp.float32)
            dscore = (prob * (dprob - delta_ref[0, s])).astype(jnp.bfloat16)
            dv_acc[keys, :] += jnp.dot(
                prob.astype(jnp.bfloat16), ds_rows[...], preferred_element_type=jnp.float32
            )
            dk_acc[keys, :] += jnp.dot(dscore, qs[...], preferred_element_type=jnp.float32)
            dqt[...] += jnp.dot(kt[c], dscore, preferred_element_type=jnp.float32)

        whole = (my_span * span) // KEYS
        last = (my_span * span + span + KEYS - 1) // KEYS
        lax.fori_loop(0, whole, lambda c, _: (block(c, False), 0)[1], 0)
        lax.fori_loop(whole, last, lambda c, _: (block(c, True), 0)[1], 0)

        dq = (dqt[...].T * inv_root).astype(jnp.bfloat16)
        for g in range(GROUPS):
            dq_ref[rows, g * HD:(g + 1) * HD] = dq[g * span:(g + 1) * span, :]
        return 0

    lax.fori_loop(0, slots, one_slot, 0)

    def back(p, _):
        dst = pl.ds(pl.multiple_of(slot_of_ref[p] * span, span), span)
        src = pl.ds(pl.multiple_of(p * span, span), span)
        dk_ref[dst, :] = (dk_acc[src, :] * inv_root).astype(dk_ref.dtype)
        dv_ref[dst, :] = dv_acc[src, :].astype(dv_ref.dtype)
        return 0

    lax.fori_loop(0, seq // span, back, 0)


def attend(slot_of, my_spans, q, d, k, v, lse, delta, span, part_type):
    rows = q.shape[0]
    seq = k.shape[0]
    kv_heads = k.shape[1] // HD
    slots = rows // span
    wide = GROUPS * span
    base = jnp.tile(jnp.arange(span, dtype=jnp.int32), GROUPS)[None, :]
    pairs = kv_heads * wide * seq * slots

    def by_head(height, width):
        return pl.BlockSpec((height, width), lambda h, *_: (0, h))

    row_terms = pl.BlockSpec((1, slots, 1, wide), lambda h, *_: (h, 0, 0, 0))
    return pl.pallas_call(
        attend_kernel,
        grid_spec=pltpu.PrefetchScalarGridSpec(
            num_scalar_prefetch=2,
            grid=(kv_heads,),
            in_specs=[
                by_head(rows, GROUPS * HD), by_head(rows, GROUPS * HD),
                by_head(seq, HD), by_head(seq, HD),
                row_terms, row_terms,
                pl.BlockSpec((1, wide), lambda h, *_: (0, 0)),
            ],
            out_specs=[by_head(rows, GROUPS * HD), by_head(seq, HD), by_head(seq, HD)],
            scratch_shapes=[
                pltpu.VMEM((seq, HD), jnp.bfloat16),
                pltpu.VMEM((seq // KEYS, HD, KEYS), jnp.bfloat16),
                pltpu.VMEM((seq, HD), jnp.bfloat16),
                pltpu.VMEM((wide, HD), jnp.bfloat16),
                pltpu.VMEM((HD, wide), jnp.bfloat16),
                pltpu.VMEM((wide, HD), jnp.bfloat16),
                pltpu.VMEM((HD, wide), jnp.bfloat16),
                pltpu.VMEM((HD, wide), jnp.float32),
                pltpu.VMEM((seq, HD), jnp.float32),
                pltpu.VMEM((seq, HD), jnp.float32),
            ],
        ),
        out_shape=[
            jax.ShapeDtypeStruct(q.shape, jnp.bfloat16),
            jax.ShapeDtypeStruct(k.shape, part_type),
            jax.ShapeDtypeStruct(k.shape, part_type),
        ],
        compiler_params=pltpu.CompilerParams(vmem_limit_bytes=48 * 2**20),
        cost_estimate=pl.CostEstimate(
            flops=7 * pairs * HD, bytes_accessed=2**24, transcendentals=pairs // 2
        ),
        name="attend",
    )(slot_of, my_spans, q, d, k, v, lse, delta, base)


def row_terms_of(terms, kv_heads, span):
    rows = terms.shape[1]
    cut = terms.reshape(kv_heads, GROUPS, rows // span, span)
    return cut.transpose(0, 2, 1, 3).reshape(kv_heads, rows // span, 1, GROUPS * span)


def per_device(query_rows, key_rows, value_rows, attn_output, log_norms, grad_output, span_order):
    own_rows = query_rows.shape[0]
    span = own_rows // 2
    ctx = lax.axis_size("ctx")
    me = lax.axis_index("ctx")
    cores = 2 if (key_rows.shape[1] // HD) % 2 == 0 and ctx % 2 == 0 else 1
    chip_groups = [[i * cores + c for c in range(cores)] for i in range(ctx // cores)]
    ring_groups = [[i * cores + c for i in range(ctx // cores)] for c in range(cores)]

    def to_heads(x, split=1, concat=0):
        if cores == 1:
            return x
        return lax.all_to_all(
            x, "ctx", split_axis=split, concat_axis=concat, axis_index_groups=chip_groups, tiled=True
        )

    q = to_heads(query_rows)
    o = to_heads(attn_output)
    lse = to_heads(log_norms, 0, 1)
    d = to_heads(lax.all_to_all(grad_output, "head", split_axis=1, concat_axis=0, tiled=True))
    kv = jnp.concatenate([to_heads(key_rows), to_heads(value_rows)], axis=1)
    kv = lax.all_gather(kv, "ctx", axis=0, axis_index_groups=ring_groups, tiled=True)
    half = kv.shape[1] // 2
    kv_heads = half // HD
    rows = q.shape[0]
    delta = jnp.sum(
        (d.astype(jnp.float32) * o.astype(jnp.float32)).reshape(rows, kv_heads * GROUPS, HD), axis=-1
    ).T
    spans = span_order.shape[0]
    slots = rows // span
    slot_of = jnp.argsort(span_order).astype(jnp.int32)
    my_spans = lax.dynamic_slice_in_dim(span_order, (me // cores) * slots, slots)
    dq, dk, dv = attend(
        slot_of, my_spans, q, d, kv[:, :half], kv[:, half:],
        row_terms_of(lse * LOG2E, kv_heads, span), row_terms_of(delta, kv_heads, span),
        span, jnp.float32,
    )
    dkv = jnp.concatenate([dk, dv], axis=1)
    dkv = lax.psum_scatter(dkv, "ctx", scatter_dimension=0, axis_index_groups=ring_groups, tiled=True)
    dkv = dkv.astype(jnp.bfloat16)
    grad_key = to_heads(dkv[:, :half], 0, 1)
    grad_value = to_heads(dkv[:, half:], 0, 1)
    dq = to_heads(dq, 0, 1)
    grad_query = lax.all_to_all(dq, "head", split_axis=0, concat_axis=1, tiled=True)
    return (grad_query, grad_key, grad_value)


def solution(mesh):
    return jax.shard_map(
        per_device,
        mesh=mesh,
        in_specs=(
            P("ctx", "head"),
            P("ctx", "head"),
            P("ctx", "head"),
            P("ctx", "head"),
            P("head", "ctx"),
            P(("ctx", "head"), None),
            P(),
        ),
        out_specs=(P(("ctx", "head"), None), P("ctx", "head"), P("ctx", "head")),
        check_vma=False,
    )
```

```python
import functools
import math

import jax
import jax.numpy as jnp
from jax import lax
from jax.experimental import pallas as pl
from jax.experimental.pallas import tpu as pltpu
from jax.sharding import PartitionSpec as P

QH = 64
KVH = 8
HD = 128
GROUPS = QH // KVH
KEYS = 256
LOG2E = math.log2(math.e)


def attend_kernel(
    slot_of_ref, my_span_ref,
    q_ref, d_ref, k_ref, v_ref, lse_ref, delta_ref, base_ref,
    dq_ref, dk_ref, dv_ref,
    ks, kt, vs, qs, qt, ds_rows, dt, dqt, dk_acc, dv_acc,
):
    span = base_ref.shape[1] // GROUPS
    seq = k_ref.shape[0]
    slots = q_ref.shape[0] // span
    inv_root = HD ** -0.5

    def place(p, _):
        src = pl.ds(pl.multiple_of(slot_of_ref[p] * span, span), span)
        dst = pl.ds(pl.multiple_of(p * span, span), span)
        ks[dst, :] = k_ref[src, :]
        vs[dst, :] = v_ref[src, :]
        return 0

    lax.fori_loop(0, seq // span, place, 0)

    def turn(c, _):
        rows = pl.ds(pl.multiple_of(c * KEYS, KEYS), KEYS)
        kt[c] = ks[rows, :].T
        dk_acc[rows, :] = jnp.zeros((KEYS, HD), jnp.float32)
        dv_acc[rows, :] = jnp.zeros((KEYS, HD), jnp.float32)
        return 0

    lax.fori_loop(0, seq // KEYS, turn, 0)

    def one_slot(s, _):
        rows = pl.ds(pl.multiple_of(s * span, span), span)
        for g in range(GROUPS):
            part = slice(g * span, (g + 1) * span)
            cols = slice(g * HD, (g + 1) * HD)
            qs[part, :] = q_ref[rows, cols]
            ds_rows[part, :] = d_ref[rows, cols]
        qt[...] = qs[...].T
        dt[...] = ds_rows[...].T
        dqt[...] = jnp.zeros_like(dqt)
        my_span = my_span_ref[s]

        def block(c, masked):
            keys = pl.ds(pl.multiple_of(c * KEYS, KEYS), KEYS)
            scores = jnp.dot(ks[keys, :], qt[...], preferred_element_type=jnp.float32)
            prob = jnp.exp2(scores * (inv_root * LOG2E) - lse_ref[0, s])
            if masked:
                key_pos = c * KEYS + lax.broadcasted_iota(jnp.int32, prob.shape, 0)
                prob = jnp.where(my_span * span + base_ref[...] >= key_pos, prob, 0.0)
            dprob = jnp.dot(vs[keys, :], dt[...], preferred_element_type=jnp.float32)
            dscore = (prob * (dprob - delta_ref[0, s])).astype(jnp.bfloat16)
            dv_acc[keys, :] += jnp.dot(
                prob.astype(jnp.bfloat16), ds_rows[...], preferred_element_type=jnp.float32
            )
            dk_acc[keys, :] += jnp.dot(dscore, qs[...], preferred_element_type=jnp.float32)
            dqt[...] += jnp.dot(kt[c], dscore, preferred_element_type=jnp.float32)

        whole = (my_span * span) // KEYS
        last = (my_span * span + span + KEYS - 1) // KEYS
        lax.fori_loop(0, whole, lambda c, _: (block(c, False), 0)[1], 0)
        lax.fori_loop(whole, last, lambda c, _: (block(c, True), 0)[1], 0)

        dq = (dqt[...].T * inv_root).astype(jnp.bfloat16)
        for g in range(GROUPS):
            dq_ref[rows, g * HD:(g + 1) * HD] = dq[g * span:(g + 1) * span, :]
        return 0

    lax.fori_loop(0, slots, one_slot, 0)

    def back(p, _):
        dst = pl.ds(pl.multiple_of(slot_of_ref[p] * span, span), span)
        src = pl.ds(pl.multiple_of(p * span, span), span)
        dk_ref[dst, :] = (dk_acc[src, :] * inv_root).astype(dk_ref.dtype)
        dv_ref[dst, :] = dv_acc[src, :].astype(dv_ref.dtype)
        return 0

    lax.fori_loop(0, seq // span, back, 0)


def attend(slot_of, my_spans, q, d, k, v, lse, delta, span, part_type):
    rows = q.shape[0]
    seq = k.shape[0]
    kv_heads = k.shape[1] // HD
    slots = rows // span
    wide = GROUPS * span
    base = jnp.tile(jnp.arange(span, dtype=jnp.int32), GROUPS)[None, :]
    pairs = kv_heads * wide * seq * slots

    def by_head(height, width):
        return pl.BlockSpec((height, width), lambda h, *_: (0, h))

    row_terms = pl.BlockSpec((1, slots, 1, wide), lambda h, *_: (h, 0, 0, 0))
    return pl.pallas_call(
        attend_kernel,
        grid_spec=pltpu.PrefetchScalarGridSpec(
            num_scalar_prefetch=2,
            grid=(kv_heads,),
            in_specs=[
                by_head(rows, GROUPS * HD), by_head(rows, GROUPS * HD),
                by_head(seq, HD), by_head(seq, HD),
                row_terms, row_terms,
                pl.BlockSpec((1, wide), lambda h, *_: (0, 0)),
            ],
            out_specs=[by_head(rows, GROUPS * HD), by_head(seq, HD), by_head(seq, HD)],
            scratch_shapes=[
                pltpu.VMEM((seq, HD), jnp.bfloat16),
                pltpu.VMEM((seq // KEYS, HD, KEYS), jnp.bfloat16),
                pltpu.VMEM((seq, HD), jnp.bfloat16),
                pltpu.VMEM((wide, HD), jnp.bfloat16),
                pltpu.VMEM((HD, wide), jnp.bfloat16),
                pltpu.VMEM((wide, HD), jnp.bfloat16),
                pltpu.VMEM((HD, wide), jnp.bfloat16),
                pltpu.VMEM((HD, wide), jnp.float32),
                pltpu.VMEM((seq, HD), jnp.float32),
                pltpu.VMEM((seq, HD), jnp.float32),
            ],
        ),
        out_shape=[
            jax.ShapeDtypeStruct(q.shape, jnp.bfloat16),
            jax.ShapeDtypeStruct(k.shape, part_type),
            jax.ShapeDtypeStruct(k.shape, part_type),
        ],
        compiler_params=pltpu.CompilerParams(vmem_limit_bytes=48 * 2**20),
        cost_estimate=pl.CostEstimate(
            flops=7 * pairs * HD, bytes_accessed=2**24, transcendentals=pairs // 2
        ),
        name="attend",
    )(slot_of, my_spans, q, d, k, v, lse, delta, base)


MESH = pl.DeviceIdType.MESH
NX = 2


def place_of():
    me = lax.axis_index("ctx")
    return me // (2 * NX), (me // 2) % NX, me % 2, lax.axis_index("head")


def device_at(z, x, core, y):
    return ((z * NX + x) * 2 + core, y)


def greet(nz, ny):
    z, x, core, y = place_of()
    barrier = pltpu.get_barrier_semaphore()

    def hello(device):
        pl.semaphore_signal(barrier, inc=1, device_id=device, device_id_type=MESH)

    for dy in range(ny):
        for dc in range(2):
            if dy or dc:
                hello(device_at(z, x, (core + dc) % 2, (y + dy) % ny))
    hello(device_at(z, 1 - x, core, y))

    @pl.when(z > 0)
    def _():
        hello(device_at(z - 1, x, core, y))

    @pl.when(z < nz - 1)
    def _():
        hello(device_at(z + 1, x, core, y))

    @pl.when((z == 0) | (z == nz - 1))
    def _():
        pl.semaphore_wait(barrier, 2 * ny + 1)

    @pl.when((z > 0) & (z < nz - 1))
    def _():
        pl.semaphore_wait(barrier, 2 * ny + 2)


def remote(src, dst, sems, index, device):
    return pltpu.make_async_remote_copy(
        src_ref=src, dst_ref=dst, send_sem=sems.at[(0, *index)], recv_sem=sems.at[(1, *index)],
        device_id=device, device_id_type=MESH,
    )


def aligned(index, size):
    return pl.ds(pl.multiple_of(index * size, size), size)


def spread_kernel(
    nz, ny, q_in, o_in, k_in, v_in, d_in, q_out, o_out, k_out, v_out, d_out,
    local_sems, pair_sems, group_sems, up_sems, down_sems, side_sems,
):
    z, x, core, y = place_of()
    other = 1 - core
    own = k_in.shape[0]
    rows = 2 * own
    share = d_in.shape[0]
    sibling = device_at(z, x, other, y)
    greet(nz, ny)

    chip_row = (z * NX + x) * rows
    mine = pl.ds(pl.multiple_of(chip_row + core * own, own), own)
    pairs, locals_ = [], []
    for n, (src, dst, where) in enumerate((
        (k_in, k_out, mine), (v_in, v_out, mine),
        (q_in, q_out, aligned(core, own)), (o_in, o_out, aligned(core, own)),
    )):
        width = dst.shape[1]
        pairs.append(remote(
            src.at[:, aligned(other, width)], dst.at[where, :], pair_sems, (n,), sibling
        ))
        locals_.append(pltpu.make_async_copy(
            src.at[:, aligned(core, width)], dst.at[where, :], local_sems.at[n]
        ))
    width = d_out.shape[1]
    group = []
    d_rows = aligned(core * ny + y, share)
    for dy in range(ny):
        for dc in range(2):
            yy, cc = (y + dy) % ny, (core + dc) % 2
            src = d_in.at[:, aligned(yy * 2 + cc, width)]
            if dy or dc:
                group.append(remote(
                    src, d_out.at[d_rows, :], group_sems, (dy, dc), device_at(z, x, cc, yy)
                ))
            else:
                locals_.append(pltpu.make_async_copy(src, d_out.at[d_rows, :], local_sems.at[4]))

    for n in range(2):
        pairs[n].start()
        locals_[n].start()
    for copy in reversed(group):
        copy.start()
    for n in range(2):
        locals_[n].wait()
        pairs[n].wait_recv()

    def hop(n, zz, sems, device):
        ref = (k_out, v_out)[n].at[aligned(zz * NX + x, rows), :]
        return remote(ref, ref, sems, (n, zz), device)

    def up(n, zz):
        return hop(n, zz, up_sems, device_at(z + 1, x, core, y))

    def down(n, zz):
        return hop(n, zz, down_sems, device_at(z - 1, x, core, y))

    def side(n, zz):
        return hop(n, zz, side_sems, device_at(z, 1 - x, core, y))

    def side_in(n, zz):
        ref = (k_out, v_out)[n].at[aligned(zz * NX + 1 - x, rows), :]
        return remote(ref, ref, side_sems, (n, zz), device_at(z, 1 - x, core, y))

    for n in range(2):
        @pl.when(z < nz - 1)
        def _():
            up(n, z).start()

        @pl.when(z > 0)
        def _():
            down(n, z).start()

        side(n, z).start()
    for n in range(2, 4):
        pairs[n].start()
        locals_[n].start()
    locals_[4].start()

    for step in range(1, nz):
        for n in range(2):
            @pl.when(z - step >= 0)
            def _():
                up(n, z - step).wait_recv()

                @pl.when(z < nz - 1)
                def _():
                    up(n, z - step).start()

                side(n, z - step).start()

            @pl.when(z + step < nz)
            def _():
                down(n, z + step).wait_recv()

                @pl.when(z > 0)
                def _():
                    down(n, z + step).start()

                side(n, z + step).start()

    for n in range(2):
        for zz in range(nz):
            side_in(n, zz).wait_recv()
            side(n, zz).wait_send()

            @pl.when((zz <= z) & (z < nz - 1))
            def _():
                up(n, zz).wait_send()

            @pl.when((zz >= z) & (z > 0))
            def _():
                down(n, zz).wait_send()

        pairs[n].wait_send()
        pairs[n + 2].wait()
        locals_[n + 2].wait()
    locals_[4].wait()
    for copy in group:
        copy.wait()


def spread(q, o, k, v, d, ctx, ny):
    nz = ctx // (2 * NX)
    rows = 2 * q.shape[0]
    seq = k.shape[0] * ctx

    def like(height, x, parts):
        return jax.ShapeDtypeStruct((height, x.shape[1] // parts), x.dtype)

    anywhere = pl.BlockSpec(memory_space=pl.ANY)
    dma = pltpu.SemaphoreType.DMA
    return pl.pallas_call(
        functools.partial(spread_kernel, nz, ny),
        out_shape=[like(rows, q, 2), like(rows, o, 2), like(seq, k, 2), like(seq, v, 2),
                   like(rows, d, 2 * ny)],
        in_specs=[anywhere] * 5,
        out_specs=[anywhere] * 5,
        scratch_shapes=[
            dma((5,)), dma((2, 4)), dma((2, ny, 2)), dma((2, 2, nz)), dma((2, 2, nz)), dma((2, 2, nz)),
        ],
        compiler_params=pltpu.CompilerParams(collective_id=0, has_side_effects=True),
        name="spread",
    )(q, o, k, v, d)


def fold_kernel(
    nz, ny, dk_in, dv_in, dq_in, gk_out, gv_out, gq_out,
    side_buf, up_buf, down_buf, out_buf, fin,
    local_sems, pair_sems, group_sems, up_sems, down_sems, side_sems,
):
    z, x, core, y = place_of()
    other = 1 - core
    rows = fin.shape[1]
    own = rows // 2
    share = gq_out.shape[0]
    parts = (dk_in, dv_in)
    greet(nz, ny)

    def side(n, zz):
        return remote(
            parts[n].at[aligned(zz * NX + 1 - x, rows), :], side_buf.at[n, zz], side_sems, (n, zz),
            device_at(z, 1 - x, core, y),
        )

    def up(n, zz):
        return remote(
            out_buf.at[n, zz], up_buf.at[n, zz], up_sems, (n, zz), device_at(z + 1, x, core, y)
        )

    def down(n, zz):
        return remote(
            out_buf.at[n, zz], down_buf.at[n, zz], down_sems, (n, zz), device_at(z - 1, x, core, y)
        )

    order = []
    for far in range(nz // 2):
        order.append(jnp.where(z < nz // 2, nz - 1 - far, far))
        order.append(jnp.where(z < nz // 2, far, nz - 1 - far))

    width = dq_in.shape[1]
    group = []
    for dy in range(ny):
        for dc in range(2):
            yy, cc = (y + dy) % ny, (core + dc) % 2
            src = dq_in.at[aligned(cc * ny + yy, share), :]
            dst = gq_out.at[:, aligned(y * 2 + core, width)]
            if dy or dc:
                group.append(remote(src, dst, group_sems, (dy, dc), device_at(z, x, cc, yy)))
            else:
                keep = pltpu.make_async_copy(src, dst, local_sems.at[2])
    for zz in order:
        for n in range(2):
            side(n, zz).start()
    for copy in reversed(group):
        copy.start()
    keep.start()

    def total(n, zz):
        mine = parts[n][aligned(zz * NX + x, rows), :].astype(jnp.float32)
        return mine + side_buf[n, zz].astype(jnp.float32)

    for zz in order:
        for n in range(2):
            @pl.when(zz > z)
            def _():
                side(n, zz).wait_recv()

                @pl.when(z == 0)
                def _():
                    out_buf[n, zz] = total(n, zz).astype(jnp.bfloat16)

                @pl.when(z > 0)
                def _():
                    up(n, zz).wait_recv()
                    out_buf[n, zz] = (
                        total(n, zz) + up_buf[n, zz].astype(jnp.float32)
                    ).astype(jnp.bfloat16)

                up(n, zz).start()

            @pl.when(zz < z)
            def _():
                side(n, zz).wait_recv()

                @pl.when(z == nz - 1)
                def _():
                    out_buf[n, zz] = total(n, zz).astype(jnp.bfloat16)

                @pl.when(z < nz - 1)
                def _():
                    down(n, zz).wait_recv()
                    out_buf[n, zz] = (
                        total(n, zz) + down_buf[n, zz].astype(jnp.float32)
                    ).astype(jnp.bfloat16)

                down(n, zz).start()

    ends = []
    for n, out in enumerate((gk_out, gv_out)):
        side(n, z).wait_recv()

        @pl.when(z == 0)
        def _():
            down(n, z).wait_recv()
            fin[n] = (total(n, z) + down_buf[n, z].astype(jnp.float32)).astype(jnp.bfloat16)

        @pl.when(z == nz - 1)
        def _():
            up(n, z).wait_recv()
            fin[n] = (total(n, z) + up_buf[n, z].astype(jnp.float32)).astype(jnp.bfloat16)

        @pl.when((z > 0) & (z < nz - 1))
        def _():
            up(n, z).wait_recv()
            down(n, z).wait_recv()
            fin[n] = (
                total(n, z) + up_buf[n, z].astype(jnp.float32) + down_buf[n, z].astype(jnp.float32)
            ).astype(jnp.bfloat16)

        columns = aligned(core, fin.shape[2])
        pair = remote(
            fin.at[n, aligned(other, own), :], out.at[:, columns], pair_sems, (n,),
            device_at(z, x, other, y),
        )
        here = pltpu.make_async_copy(
            fin.at[n, aligned(core, own), :], out.at[:, columns], local_sems.at[n]
        )
        pair.start()
        here.start()
        ends += [pair, here]

    for copy in ends + group + [keep]:
        copy.wait()
    for n in range(2):
        for zz in range(nz):
            side(n, zz).wait_send()

            @pl.when(zz > z)
            def _():
                up(n, zz).wait_send()

            @pl.when(zz < z)
            def _():
                down(n, zz).wait_send()


def fold(dk, dv, dq, ctx, ny):
    nz = ctx // (2 * NX)
    rows = dq.shape[0]
    own = rows // 2
    width = dk.shape[1]
    anywhere = pl.BlockSpec(memory_space=pl.ANY)
    whole = pl.BlockSpec(memory_space=pltpu.VMEM)
    dma = pltpu.SemaphoreType.DMA
    buffers = pltpu.VMEM((2, nz, rows, width), jnp.bfloat16)
    kv_out = jax.ShapeDtypeStruct((own, 2 * width), jnp.bfloat16)
    return pl.pallas_call(
        functools.partial(fold_kernel, nz, ny),
        out_shape=[kv_out, kv_out,
                   jax.ShapeDtypeStruct((rows // (2 * ny), dq.shape[1] * 2 * ny), jnp.bfloat16)],
        in_specs=[whole, whole, anywhere],
        out_specs=[anywhere] * 3,
        scratch_shapes=[
            buffers, buffers, buffers, buffers, pltpu.VMEM((2, rows, width), jnp.bfloat16),
            dma((3,)), dma((2, 2)), dma((2, ny, 2)), dma((2, 2, nz)), dma((2, 2, nz)), dma((2, 2, nz)),
        ],
        compiler_params=pltpu.CompilerParams(
            collective_id=1, has_side_effects=True, vmem_limit_bytes=32 * 2**20
        ),
        name="fold",
    )(dk, dv, dq)


def row_terms_of(terms, kv_heads, span):
    rows = terms.shape[1]
    cut = terms.reshape(kv_heads, GROUPS, rows // span, span)
    return cut.transpose(0, 2, 1, 3).reshape(kv_heads, rows // span, 1, GROUPS * span)


def per_device(query_rows, key_rows, value_rows, attn_output, log_norms, grad_output, span_order):
    own_rows = query_rows.shape[0]
    span = own_rows // 2
    ctx = lax.axis_size("ctx")
    me = lax.axis_index("ctx")
    cores = 2 if (key_rows.shape[1] // HD) % 2 == 0 and ctx % 2 == 0 else 1
    chip_groups = [[i * cores + c for c in range(cores)] for i in range(ctx // cores)]
    ring_groups = [[i * cores + c for i in range(ctx // cores)] for c in range(cores)]

    def to_heads(x, split=1, concat=0):
        if cores == 1:
            return x
        return lax.all_to_all(
            x, "ctx", split_axis=split, concat_axis=concat, axis_index_groups=chip_groups, tiled=True
        )

    ny = lax.axis_size("head")
    by_kernels = cores == 2 and ctx % (4 * NX) == 0
    lse = to_heads(log_norms, 0, 1)
    if by_kernels:
        q, o, k, v, d = spread(query_rows, attn_output, key_rows, value_rows, grad_output, ctx, ny)
    else:
        q = to_heads(query_rows)
        o = to_heads(attn_output)
        d = to_heads(lax.all_to_all(grad_output, "head", split_axis=1, concat_axis=0, tiled=True))
        kv = jnp.concatenate([to_heads(key_rows), to_heads(value_rows)], axis=1)
        kv = lax.all_gather(kv, "ctx", axis=0, axis_index_groups=ring_groups, tiled=True)
        k, v = kv[:, :kv.shape[1] // 2], kv[:, kv.shape[1] // 2:]
    half = k.shape[1]
    kv_heads = half // HD
    rows = q.shape[0]
    delta = jnp.sum(
        (d.astype(jnp.float32) * o.astype(jnp.float32)).reshape(rows, kv_heads * GROUPS, HD), axis=-1
    ).T
    spans = span_order.shape[0]
    slots = rows // span
    slot_of = jnp.argsort(span_order).astype(jnp.int32)
    my_spans = lax.dynamic_slice_in_dim(span_order, (me // cores) * slots, slots)
    dq, dk, dv = attend(
        slot_of, my_spans, q, d, k, v,
        row_terms_of(lse * LOG2E, kv_heads, span), row_terms_of(delta, kv_heads, span),
        span, jnp.bfloat16 if by_kernels else jnp.float32,
    )
    if by_kernels:
        return tuple(fold(dk, dv, dq, ctx, ny)[n] for n in (2, 0, 1))
    dkv = jnp.concatenate([dk, dv], axis=1)
    dkv = lax.psum_scatter(dkv, "ctx", scatter_dimension=0, axis_index_groups=ring_groups, tiled=True)
    dkv = dkv.astype(jnp.bfloat16)
    grad_key = to_heads(dkv[:, :half], 0, 1)
    grad_value = to_heads(dkv[:, half:], 0, 1)
    dq = to_heads(dq, 0, 1)
    grad_query = lax.all_to_all(dq, "head", split_axis=0, concat_axis=1, tiled=True)
    return (grad_query, grad_key, grad_value)


def solution(mesh):
    return jax.shard_map(
        per_device,
        mesh=mesh,
        in_specs=(
            P("ctx", "head"),
            P("ctx", "head"),
            P("ctx", "head"),
            P("ctx", "head"),
            P("head", "ctx"),
            P(("ctx", "head"), None),
            P(),
        ),
        out_specs=(P(("ctx", "head"), None), P("ctx", "head"), P("ctx", "head")),
        check_vma=False,
    )
```

```python
import functools
import math

import jax
import jax.numpy as jnp
from jax import lax
from jax.experimental import pallas as pl
from jax.experimental.pallas import tpu as pltpu
from jax.sharding import PartitionSpec as P

QH = 64
KVH = 8
HD = 128
GROUPS = QH // KVH
KEYS = 256
LOG2E = math.log2(math.e)


def attend_kernel(
    slot_of_ref, my_span_ref,
    q_ref, d_ref, k_ref, v_ref, lse_ref, delta_ref, base_ref,
    dq_ref, dk_ref, dv_ref,
    ks, kt, vs, qs, qt, ds_rows, dt, dqt, dk_acc, dv_acc,
):
    span = base_ref.shape[1] // GROUPS
    seq = k_ref.shape[0]
    slots = q_ref.shape[0] // span
    inv_root = HD ** -0.5

    def place(p, _):
        src = pl.ds(pl.multiple_of(slot_of_ref[p] * span, span), span)
        dst = pl.ds(pl.multiple_of(p * span, span), span)
        ks[dst, :] = k_ref[src, :]
        vs[dst, :] = v_ref[src, :]
        return 0

    lax.fori_loop(0, seq // span, place, 0)

    def turn(c, _):
        rows = pl.ds(pl.multiple_of(c * KEYS, KEYS), KEYS)
        kt[c] = ks[rows, :].T
        dk_acc[rows, :] = jnp.zeros((KEYS, HD), jnp.float32)
        dv_acc[rows, :] = jnp.zeros((KEYS, HD), jnp.float32)
        return 0

    lax.fori_loop(0, seq // KEYS, turn, 0)

    def one_slot(s, _):
        rows = pl.ds(pl.multiple_of(s * span, span), span)
        for g in range(GROUPS):
            part = slice(g * span, (g + 1) * span)
            cols = slice(g * HD, (g + 1) * HD)
            qs[part, :] = q_ref[rows, cols]
            ds_rows[part, :] = d_ref[rows, cols]
        qt[...] = qs[...].T
        dt[...] = ds_rows[...].T
        dqt[...] = jnp.zeros_like(dqt)
        my_span = my_span_ref[s]

        def block(c, masked, size=1):
            keys = pl.ds(pl.multiple_of(c * KEYS, KEYS), size * KEYS)
            scores = jnp.dot(ks[keys, :], qt[...], preferred_element_type=jnp.float32)
            prob = jnp.exp2(scores * (inv_root * LOG2E) - lse_ref[0, s])
            if masked:
                key_pos = c * KEYS + lax.broadcasted_iota(jnp.int32, prob.shape, 0)
                prob = jnp.where(my_span * span + base_ref[...] >= key_pos, prob, 0.0)
            dprob = jnp.dot(vs[keys, :], dt[...], preferred_element_type=jnp.float32)
            dscore = (prob * (dprob - delta_ref[0, s])).astype(jnp.bfloat16)
            dv_acc[keys, :] += jnp.dot(
                prob.astype(jnp.bfloat16), ds_rows[...], preferred_element_type=jnp.float32
            )
            dk_acc[keys, :] += jnp.dot(dscore, qs[...], preferred_element_type=jnp.float32)
            dqt[...] += sum(
                jnp.dot(kt[c + i], dscore[i * KEYS:(i + 1) * KEYS], preferred_element_type=jnp.float32)
                for i in range(size)
            )

        whole = (my_span * span) // KEYS
        last = (my_span * span + span + KEYS - 1) // KEYS
        lax.fori_loop(0, whole // 2, lambda c, _: (block(2 * c, False, 2), 0)[1], 0)

        @pl.when(whole % 2 == 1)
        def _():
            block(whole - 1, False)

        lax.fori_loop(whole, last, lambda c, _: (block(c, True), 0)[1], 0)

        dq = (dqt[...].T * inv_root).astype(jnp.bfloat16)
        for g in range(GROUPS):
            dq_ref[rows, g * HD:(g + 1) * HD] = dq[g * span:(g + 1) * span, :]
        return 0

    lax.fori_loop(0, slots, one_slot, 0)

    def back(p, _):
        dst = pl.ds(pl.multiple_of(slot_of_ref[p] * span, span), span)
        src = pl.ds(pl.multiple_of(p * span, span), span)
        dk_ref[dst, :] = (dk_acc[src, :] * inv_root).astype(dk_ref.dtype)
        dv_ref[dst, :] = dv_acc[src, :].astype(dv_ref.dtype)
        return 0

    lax.fori_loop(0, seq // span, back, 0)


def attend(slot_of, my_spans, q, d, k, v, lse, delta, span, part_type):
    rows = q.shape[0]
    seq = k.shape[0]
    kv_heads = k.shape[1] // HD
    slots = rows // span
    wide = GROUPS * span
    base = jnp.tile(jnp.arange(span, dtype=jnp.int32), GROUPS)[None, :]
    pairs = kv_heads * wide * seq * slots

    def by_head(height, width):
        return pl.BlockSpec((height, width), lambda h, *_: (0, h))

    row_terms = pl.BlockSpec((1, slots, 1, wide), lambda h, *_: (h, 0, 0, 0))
    return pl.pallas_call(
        attend_kernel,
        grid_spec=pltpu.PrefetchScalarGridSpec(
            num_scalar_prefetch=2,
            grid=(kv_heads,),
            in_specs=[
                by_head(rows, GROUPS * HD), by_head(rows, GROUPS * HD),
                by_head(seq, HD), by_head(seq, HD),
                row_terms, row_terms,
                pl.BlockSpec((1, wide), lambda h, *_: (0, 0)),
            ],
            out_specs=[by_head(rows, GROUPS * HD), by_head(seq, HD), by_head(seq, HD)],
            scratch_shapes=[
                pltpu.VMEM((seq, HD), jnp.bfloat16),
                pltpu.VMEM((seq // KEYS, HD, KEYS), jnp.bfloat16),
                pltpu.VMEM((seq, HD), jnp.bfloat16),
                pltpu.VMEM((wide, HD), jnp.bfloat16),
                pltpu.VMEM((HD, wide), jnp.bfloat16),
                pltpu.VMEM((wide, HD), jnp.bfloat16),
                pltpu.VMEM((HD, wide), jnp.bfloat16),
                pltpu.VMEM((HD, wide), jnp.float32),
                pltpu.VMEM((seq, HD), jnp.float32),
                pltpu.VMEM((seq, HD), jnp.float32),
            ],
        ),
        out_shape=[
            jax.ShapeDtypeStruct(q.shape, jnp.bfloat16),
            jax.ShapeDtypeStruct(k.shape, part_type),
            jax.ShapeDtypeStruct(k.shape, part_type),
        ],
        compiler_params=pltpu.CompilerParams(vmem_limit_bytes=48 * 2**20),
        cost_estimate=pl.CostEstimate(
            flops=7 * pairs * HD, bytes_accessed=2**24, transcendentals=pairs // 2
        ),
        name="attend",
    )(slot_of, my_spans, q, d, k, v, lse, delta, base)


MESH = pl.DeviceIdType.MESH
NX = 2


def place_of():
    me = lax.axis_index("ctx")
    return me // (2 * NX), (me // 2) % NX, me % 2, lax.axis_index("head")


def device_at(z, x, core, y):
    return ((z * NX + x) * 2 + core, y)


def greet(nz, ny):
    z, x, core, y = place_of()
    barrier = pltpu.get_barrier_semaphore()

    def hello(device):
        pl.semaphore_signal(barrier, inc=1, device_id=device, device_id_type=MESH)

    for dy in range(ny):
        for dc in range(2):
            if dy or dc:
                hello(device_at(z, x, (core + dc) % 2, (y + dy) % ny))
    hello(device_at(z, 1 - x, core, y))

    @pl.when(z > 0)
    def _():
        hello(device_at(z - 1, x, core, y))

    @pl.when(z < nz - 1)
    def _():
        hello(device_at(z + 1, x, core, y))

    @pl.when((z == 0) | (z == nz - 1))
    def _():
        pl.semaphore_wait(barrier, 2 * ny + 1)

    @pl.when((z > 0) & (z < nz - 1))
    def _():
        pl.semaphore_wait(barrier, 2 * ny + 2)


def remote(src, dst, sems, index, device):
    return pltpu.make_async_remote_copy(
        src_ref=src, dst_ref=dst, send_sem=sems.at[(0, *index)], recv_sem=sems.at[(1, *index)],
        device_id=device, device_id_type=MESH,
    )


def aligned(index, size):
    return pl.ds(pl.multiple_of(index * size, size), size)


def spread_kernel(
    nz, ny, q_in, o_in, k_in, v_in, d_in, l_in, q_out, o_out, k_out, v_out, d_out, l_out,
    local_sems, pair_sems, group_sems, up_sems, down_sems, side_sems,
):
    z, x, core, y = place_of()
    other = 1 - core
    own = k_in.shape[0]
    rows = 2 * own
    share = d_in.shape[0]
    sibling = device_at(z, x, other, y)
    greet(nz, ny)

    chip_row = (z * NX + x) * rows
    mine = pl.ds(pl.multiple_of(chip_row + core * own, own), own)
    pairs, locals_ = [], []
    for n, (src, dst, where) in enumerate((
        (k_in, k_out, mine), (v_in, v_out, mine),
        (q_in, q_out, aligned(core, own)), (o_in, o_out, aligned(core, own)),
    )):
        width = dst.shape[1]
        pairs.append(remote(
            src.at[:, aligned(other, width)], dst.at[where, :], pair_sems, (n,), sibling
        ))
        locals_.append(pltpu.make_async_copy(
            src.at[:, aligned(core, width)], dst.at[where, :], local_sems.at[n]
        ))
    width = d_out.shape[1]
    group = []
    d_rows = aligned(core * ny + y, share)
    for dy in range(ny):
        for dc in range(2):
            yy, cc = (y + dy) % ny, (core + dc) % 2
            src = d_in.at[:, aligned(yy * 2 + cc, width)]
            if dy or dc:
                group.append(remote(
                    src, d_out.at[d_rows, :], group_sems, (dy, dc), device_at(z, x, cc, yy)
                ))
            else:
                locals_.append(pltpu.make_async_copy(src, d_out.at[d_rows, :], local_sems.at[4]))

    heads = l_out.shape[1]
    pairs.append(remote(l_in.at[aligned(other, heads), :], l_out.at[core], pair_sems, (4,), sibling))
    lse_copy = pltpu.make_async_copy(
        l_in.at[aligned(core, heads), :], l_out.at[core], local_sems.at[5]
    )

    for n in range(2):
        pairs[n].start()
        locals_[n].start()
    for n in range(2):
        locals_[n].wait()
        pairs[n].wait_recv()

    def hop(n, zz, sems, device):
        ref = (k_out, v_out)[n].at[aligned(zz * NX + x, rows), :]
        return remote(ref, ref, sems, (n, zz), device)

    def up(n, zz):
        return hop(n, zz, up_sems, device_at(z + 1, x, core, y))

    def down(n, zz):
        return hop(n, zz, down_sems, device_at(z - 1, x, core, y))

    def side(n, zz):
        return hop(n, zz, side_sems, device_at(z, 1 - x, core, y))

    def side_in(n, zz):
        ref = (k_out, v_out)[n].at[aligned(zz * NX + 1 - x, rows), :]
        return remote(ref, ref, side_sems, (n, zz), device_at(z, 1 - x, core, y))

    for n in range(2):
        @pl.when(z < nz - 1)
        def _():
            up(n, z).start()

        @pl.when(z > 0)
        def _():
            down(n, z).start()

        side(n, z).start()
    for copy in reversed(group):
        copy.start()
    for n in range(2, 4):
        pairs[n].start()
        locals_[n].start()
    locals_[4].start()
    pairs[4].start()
    lse_copy.start()

    for step in range(1, nz):
        for n in range(2):
            @pl.when(z - step >= 0)
            def _():
                up(n, z - step).wait_recv()

                @pl.when(z < nz - 1)
                def _():
                    up(n, z - step).start()

                side(n, z - step).start()

            @pl.when(z + step < nz)
            def _():
                down(n, z + step).wait_recv()

                @pl.when(z > 0)
                def _():
                    down(n, z + step).start()

                side(n, z + step).start()

    for n in range(2):
        for zz in range(nz):
            side_in(n, zz).wait_recv()
            side(n, zz).wait_send()

            @pl.when((zz <= z) & (z < nz - 1))
            def _():
                up(n, zz).wait_send()

            @pl.when((zz >= z) & (z > 0))
            def _():
                down(n, zz).wait_send()

        pairs[n].wait_send()
        pairs[n + 2].wait()
        locals_[n + 2].wait()
    locals_[4].wait()
    pairs[4].wait()
    lse_copy.wait()
    for copy in group:
        copy.wait()


def spread(q, o, k, v, d, lse, ctx, ny):
    nz = ctx // (2 * NX)
    rows = 2 * q.shape[0]
    seq = k.shape[0] * ctx

    def like(height, x, parts):
        return jax.ShapeDtypeStruct((height, x.shape[1] // parts), x.dtype)

    anywhere = pl.BlockSpec(memory_space=pl.ANY)
    dma = pltpu.SemaphoreType.DMA
    return pl.pallas_call(
        functools.partial(spread_kernel, nz, ny),
        out_shape=[like(rows, q, 2), like(rows, o, 2), like(seq, k, 2), like(seq, v, 2),
                   like(rows, d, 2 * ny),
                   jax.ShapeDtypeStruct((2, lse.shape[0] // 2, lse.shape[1]), lse.dtype)],
        in_specs=[anywhere] * 6,
        out_specs=[anywhere] * 6,
        scratch_shapes=[
            dma((6,)), dma((2, 5)), dma((2, ny, 2)), dma((2, 2, nz)), dma((2, 2, nz)), dma((2, 2, nz)),
        ],
        compiler_params=pltpu.CompilerParams(collective_id=0, has_side_effects=True),
        name="spread",
    )(q, o, k, v, d, lse)


def fold_kernel(
    nz, ny, dk_in, dv_in, dq_in, gk_out, gv_out, gq_out,
    side_buf, up_buf, down_buf, out_buf, fin,
    local_sems, pair_sems, group_sems, up_sems, down_sems, side_sems,
):
    z, x, core, y = place_of()
    other = 1 - core
    rows = fin.shape[1]
    own = rows // 2
    share = gq_out.shape[0]
    parts = (dk_in, dv_in)
    greet(nz, ny)

    def side(n, zz):
        return remote(
            parts[n].at[aligned(zz * NX + 1 - x, rows), :], side_buf.at[n, zz], side_sems, (n, zz),
            device_at(z, 1 - x, core, y),
        )

    def up(n, zz):
        return remote(
            out_buf.at[n, zz], up_buf.at[n, zz], up_sems, (n, zz), device_at(z + 1, x, core, y)
        )

    def down(n, zz):
        return remote(
            out_buf.at[n, zz], down_buf.at[n, zz], down_sems, (n, zz), device_at(z - 1, x, core, y)
        )

    order = []
    for far in range(nz // 2):
        order.append(jnp.where(z < nz // 2, nz - 1 - far, far))
        order.append(jnp.where(z < nz // 2, far, nz - 1 - far))

    width = dq_in.shape[1]
    group = []
    for dy in range(ny):
        for dc in range(2):
            yy, cc = (y + dy) % ny, (core + dc) % 2
            src = dq_in.at[aligned(cc * ny + yy, share), :]
            dst = gq_out.at[:, aligned(y * 2 + core, width)]
            if dy or dc:
                group.append(remote(src, dst, group_sems, (dy, dc), device_at(z, x, cc, yy)))
            else:
                keep = pltpu.make_async_copy(src, dst, local_sems.at[2])
    for zz in order:
        for n in range(2):
            side(n, zz).start()
    for copy in reversed(group):
        copy.start()
    keep.start()

    def total(n, zz):
        mine = parts[n][aligned(zz * NX + x, rows), :].astype(jnp.float32)
        return mine + side_buf[n, zz].astype(jnp.float32)

    for zz in order:
        for n in range(2):
            @pl.when(zz > z)
            def _():
                side(n, zz).wait_recv()

                @pl.when(z == 0)
                def _():
                    out_buf[n, zz] = total(n, zz).astype(jnp.bfloat16)

                @pl.when(z > 0)
                def _():
                    up(n, zz).wait_recv()
                    out_buf[n, zz] = (
                        total(n, zz) + up_buf[n, zz].astype(jnp.float32)
                    ).astype(jnp.bfloat16)

                up(n, zz).start()

            @pl.when(zz < z)
            def _():
                side(n, zz).wait_recv()

                @pl.when(z == nz - 1)
                def _():
                    out_buf[n, zz] = total(n, zz).astype(jnp.bfloat16)

                @pl.when(z < nz - 1)
                def _():
                    down(n, zz).wait_recv()
                    out_buf[n, zz] = (
                        total(n, zz) + down_buf[n, zz].astype(jnp.float32)
                    ).astype(jnp.bfloat16)

                down(n, zz).start()

    ends = []
    for n, out in enumerate((gk_out, gv_out)):
        side(n, z).wait_recv()

        @pl.when(z == 0)
        def _():
            down(n, z).wait_recv()
            fin[n] = (total(n, z) + down_buf[n, z].astype(jnp.float32)).astype(jnp.bfloat16)

        @pl.when(z == nz - 1)
        def _():
            up(n, z).wait_recv()
            fin[n] = (total(n, z) + up_buf[n, z].astype(jnp.float32)).astype(jnp.bfloat16)

        @pl.when((z > 0) & (z < nz - 1))
        def _():
            up(n, z).wait_recv()
            down(n, z).wait_recv()
            fin[n] = (
                total(n, z) + up_buf[n, z].astype(jnp.float32) + down_buf[n, z].astype(jnp.float32)
            ).astype(jnp.bfloat16)

        columns = aligned(core, fin.shape[2])
        pair = remote(
            fin.at[n, aligned(other, own), :], out.at[:, columns], pair_sems, (n,),
            device_at(z, x, other, y),
        )
        here = pltpu.make_async_copy(
            fin.at[n, aligned(core, own), :], out.at[:, columns], local_sems.at[n]
        )
        pair.start()
        here.start()
        ends += [pair, here]

    for copy in ends + group + [keep]:
        copy.wait()
    for n in range(2):
        for zz in range(nz):
            side(n, zz).wait_send()

            @pl.when(zz > z)
            def _():
                up(n, zz).wait_send()

            @pl.when(zz < z)
            def _():
                down(n, zz).wait_send()


def fold(dk, dv, dq, ctx, ny):
    nz = ctx // (2 * NX)
    rows = dq.shape[0]
    own = rows // 2
    width = dk.shape[1]
    anywhere = pl.BlockSpec(memory_space=pl.ANY)
    whole = pl.BlockSpec(memory_space=pltpu.VMEM)
    dma = pltpu.SemaphoreType.DMA
    buffers = pltpu.VMEM((2, nz, rows, width), jnp.bfloat16)
    kv_out = jax.ShapeDtypeStruct((own, 2 * width), jnp.bfloat16)
    return pl.pallas_call(
        functools.partial(fold_kernel, nz, ny),
        out_shape=[kv_out, kv_out,
                   jax.ShapeDtypeStruct((rows // (2 * ny), dq.shape[1] * 2 * ny), jnp.bfloat16)],
        in_specs=[whole, whole, anywhere],
        out_specs=[anywhere] * 3,
        scratch_shapes=[
            buffers, buffers, buffers, buffers, pltpu.VMEM((2, rows, width), jnp.bfloat16),
            dma((3,)), dma((2, 2)), dma((2, ny, 2)), dma((2, 2, nz)), dma((2, 2, nz)), dma((2, 2, nz)),
        ],
        compiler_params=pltpu.CompilerParams(
            collective_id=1, has_side_effects=True, vmem_limit_bytes=32 * 2**20
        ),
        name="fold",
    )(dk, dv, dq)


def row_terms_of(terms, kv_heads, span):
    rows = terms.shape[1]
    cut = terms.reshape(kv_heads, GROUPS, rows // span, span)
    return cut.transpose(0, 2, 1, 3).reshape(kv_heads, rows // span, 1, GROUPS * span)


def per_device(query_rows, key_rows, value_rows, attn_output, log_norms, grad_output, span_order):
    own_rows = query_rows.shape[0]
    span = own_rows // 2
    ctx = lax.axis_size("ctx")
    me = lax.axis_index("ctx")
    cores = 2 if (key_rows.shape[1] // HD) % 2 == 0 and ctx % 2 == 0 else 1
    chip_groups = [[i * cores + c for c in range(cores)] for i in range(ctx // cores)]
    ring_groups = [[i * cores + c for i in range(ctx // cores)] for c in range(cores)]

    def to_heads(x, split=1, concat=0):
        if cores == 1:
            return x
        return lax.all_to_all(
            x, "ctx", split_axis=split, concat_axis=concat, axis_index_groups=chip_groups, tiled=True
        )

    ny = lax.axis_size("head")
    by_kernels = cores == 2 and ctx % (4 * NX) == 0
    if by_kernels:
        q, o, k, v, d, lse = spread(
            query_rows, attn_output, key_rows, value_rows, grad_output, log_norms, ctx, ny
        )
        lse = jnp.concatenate([lse[0], lse[1]], axis=1)
    else:
        lse = to_heads(log_norms, 0, 1)
        q = to_heads(query_rows)
        o = to_heads(attn_output)
        d = to_heads(lax.all_to_all(grad_output, "head", split_axis=1, concat_axis=0, tiled=True))
        kv = jnp.concatenate([to_heads(key_rows), to_heads(value_rows)], axis=1)
        kv = lax.all_gather(kv, "ctx", axis=0, axis_index_groups=ring_groups, tiled=True)
        k, v = kv[:, :kv.shape[1] // 2], kv[:, kv.shape[1] // 2:]
    half = k.shape[1]
    kv_heads = half // HD
    rows = q.shape[0]
    delta = jnp.sum(
        (d.astype(jnp.float32) * o.astype(jnp.float32)).reshape(rows, kv_heads * GROUPS, HD), axis=-1
    ).T
    spans = span_order.shape[0]
    slots = rows // span
    ids = jnp.arange(spans, dtype=jnp.int32)
    slot_of = jnp.sum(jnp.where(span_order[None, :] == ids[:, None], ids[None, :], 0), axis=1)
    my_spans = lax.dynamic_slice_in_dim(span_order, (me // cores) * slots, slots)
    dq, dk, dv = attend(
        slot_of, my_spans, q, d, k, v,
        row_terms_of(lse * LOG2E, kv_heads, span), row_terms_of(delta, kv_heads, span),
        span, jnp.bfloat16 if by_kernels else jnp.float32,
    )
    if by_kernels:
        grad_key, grad_value, grad_query = fold(dk, dv, dq, ctx, ny)
        return (grad_query, grad_key, grad_value)
    dkv = jnp.concatenate([dk, dv], axis=1)
    dkv = lax.psum_scatter(dkv, "ctx", scatter_dimension=0, axis_index_groups=ring_groups, tiled=True)
    dkv = dkv.astype(jnp.bfloat16)
    grad_key = to_heads(dkv[:, :half], 0, 1)
    grad_value = to_heads(dkv[:, half:], 0, 1)
    dq = to_heads(dq, 0, 1)
    grad_query = lax.all_to_all(dq, "head", split_axis=0, concat_axis=1, tiled=True)
    return (grad_query, grad_key, grad_value)


def solution(mesh):
    return jax.shard_map(
        per_device,
        mesh=mesh,
        in_specs=(
            P("ctx", "head"),
            P("ctx", "head"),
            P("ctx", "head"),
            P("ctx", "head"),
            P("head", "ctx"),
            P(("ctx", "head"), None),
            P(),
        ),
        out_specs=(P(("ctx", "head"), None), P("ctx", "head"), P("ctx", "head")),
        check_vma=False,
    )
```

```python
import functools
import math

import jax
import jax.numpy as jnp
from jax import lax
from jax.experimental import pallas as pl
from jax.experimental.pallas import tpu as pltpu
from jax.sharding import PartitionSpec as P

QH = 64
KVH = 8
HD = 128
GROUPS = QH // KVH
KEYS = 256
LOG2E = math.log2(math.e)


def attend_kernel(
    slot_of_ref, my_span_ref,
    q_ref, d_ref, k_ref, v_ref, lse_ref, delta_ref, base_ref,
    dq_ref, dk_ref, dv_ref,
    ks, kt, vs, qs, qt, ds_rows, dt, dqt, dk_acc, dv_acc,
):
    span = base_ref.shape[1] // GROUPS
    seq = k_ref.shape[0]
    slots = q_ref.shape[0] // span
    inv_root = HD ** -0.5

    def place(p, _):
        src = pl.ds(pl.multiple_of(slot_of_ref[p] * span, span), span)
        dst = pl.ds(pl.multiple_of(p * span, span), span)
        ks[dst, :] = k_ref[src, :]
        vs[dst, :] = v_ref[src, :]
        return 0

    lax.fori_loop(0, seq // span, place, 0)

    def turn(c, _):
        rows = pl.ds(pl.multiple_of(c * KEYS, KEYS), KEYS)
        kt[c] = ks[rows, :].T
        dk_acc[rows, :] = jnp.zeros((KEYS, HD), jnp.float32)
        dv_acc[rows, :] = jnp.zeros((KEYS, HD), jnp.float32)
        return 0

    lax.fori_loop(0, seq // KEYS, turn, 0)

    def one_slot(s, _):
        rows = pl.ds(pl.multiple_of(s * span, span), span)
        for g in range(GROUPS):
            part = slice(g * span, (g + 1) * span)
            cols = slice(g * HD, (g + 1) * HD)
            qs[part, :] = q_ref[rows, cols]
            ds_rows[part, :] = d_ref[rows, cols]
        qt[...] = qs[...].T
        dt[...] = ds_rows[...].T
        dqt[...] = jnp.zeros_like(dqt)
        my_span = my_span_ref[s]

        def block(c, masked, size=1):
            wide = qt.shape[1]
            cuts = [slice(j, min(j + KEYS, wide)) for j in range(0, wide, KEYS)]
            tiles = [(i, cut) for i in range(size) for cut in cuts]

            def keys_of(i):
                return pl.ds(pl.multiple_of((c + i) * KEYS, KEYS), KEYS)

            def products(i, cut):
                scores = jnp.dot(ks[keys_of(i), :], qt[:, cut], preferred_element_type=jnp.float32)
                dprob = jnp.dot(vs[keys_of(i), :], dt[:, cut], preferred_element_type=jnp.float32)
                return scores, dprob

            probs, dscores = [], []
            ahead = products(*tiles[0])
            for n, (i, cut) in enumerate(tiles):
                scores, dprob = ahead
                if n + 1 < len(tiles):
                    ahead = products(*tiles[n + 1])
                prob = jnp.exp2(scores * (inv_root * LOG2E) - lse_ref[0, s][:, cut])
                if masked:
                    key_pos = (c + i) * KEYS + lax.broadcasted_iota(jnp.int32, prob.shape, 0)
                    prob = jnp.where(my_span * span + base_ref[:, cut] >= key_pos, prob, 0.0)
                dscores.append((prob * (dprob - delta_ref[0, s][:, cut])).astype(jnp.bfloat16))
                probs.append(prob.astype(jnp.bfloat16))
                if cut is cuts[-1]:
                    prob_low = jnp.concatenate(probs[-len(cuts):], axis=1)
                    dscore = jnp.concatenate(dscores[-len(cuts):], axis=1)
                    dv_acc[keys_of(i), :] += jnp.dot(
                        prob_low, ds_rows[...], preferred_element_type=jnp.float32
                    )
                    dk_acc[keys_of(i), :] += jnp.dot(
                        dscore, qs[...], preferred_element_type=jnp.float32
                    )
                    dqt[...] += jnp.dot(kt[c + i], dscore, preferred_element_type=jnp.float32)

        whole = (my_span * span) // KEYS
        last = (my_span * span + span + KEYS - 1) // KEYS
        lax.fori_loop(0, whole // 2, lambda c, _: (block(2 * c, False, 2), 0)[1], 0)

        @pl.when(whole % 2 == 1)
        def _():
            block(whole - 1, False)

        lax.fori_loop(whole, last, lambda c, _: (block(c, True), 0)[1], 0)

        dq = (dqt[...].T * inv_root).astype(jnp.bfloat16)
        for g in range(GROUPS):
            dq_ref[rows, g * HD:(g + 1) * HD] = dq[g * span:(g + 1) * span, :]
        return 0

    lax.fori_loop(0, slots, one_slot, 0)

    def back(p, _):
        dst = pl.ds(pl.multiple_of(slot_of_ref[p] * span, span), span)
        src = pl.ds(pl.multiple_of(p * span, span), span)
        dk_ref[dst, :] = (dk_acc[src, :] * inv_root).astype(dk_ref.dtype)
        dv_ref[dst, :] = dv_acc[src, :].astype(dv_ref.dtype)
        return 0

    lax.fori_loop(0, seq // span, back, 0)


def attend(slot_of, my_spans, q, d, k, v, lse, delta, span, part_type):
    rows = q.shape[0]
    seq = k.shape[0]
    kv_heads = k.shape[1] // HD
    slots = rows // span
    wide = GROUPS * span
    base = jnp.tile(jnp.arange(span, dtype=jnp.int32), GROUPS)[None, :]
    pairs = kv_heads * wide * seq * slots

    def by_head(height, width):
        return pl.BlockSpec((height, width), lambda h, *_: (0, h))

    row_terms = pl.BlockSpec((1, slots, 1, wide), lambda h, *_: (h, 0, 0, 0))
    return pl.pallas_call(
        attend_kernel,
        grid_spec=pltpu.PrefetchScalarGridSpec(
            num_scalar_prefetch=2,
            grid=(kv_heads,),
            in_specs=[
                by_head(rows, GROUPS * HD), by_head(rows, GROUPS * HD),
                by_head(seq, HD), by_head(seq, HD),
                row_terms, row_terms,
                pl.BlockSpec((1, wide), lambda h, *_: (0, 0)),
            ],
            out_specs=[by_head(rows, GROUPS * HD), by_head(seq, HD), by_head(seq, HD)],
            scratch_shapes=[
                pltpu.VMEM((seq, HD), jnp.bfloat16),
                pltpu.VMEM((seq // KEYS, HD, KEYS), jnp.bfloat16),
                pltpu.VMEM((seq, HD), jnp.bfloat16),
                pltpu.VMEM((wide, HD), jnp.bfloat16),
                pltpu.VMEM((HD, wide), jnp.bfloat16),
                pltpu.VMEM((wide, HD), jnp.bfloat16),
                pltpu.VMEM((HD, wide), jnp.bfloat16),
                pltpu.VMEM((HD, wide), jnp.float32),
                pltpu.VMEM((seq, HD), jnp.float32),
                pltpu.VMEM((seq, HD), jnp.float32),
            ],
        ),
        out_shape=[
            jax.ShapeDtypeStruct(q.shape, jnp.bfloat16),
            jax.ShapeDtypeStruct(k.shape, part_type),
            jax.ShapeDtypeStruct(k.shape, part_type),
        ],
        compiler_params=pltpu.CompilerParams(vmem_limit_bytes=48 * 2**20),
        cost_estimate=pl.CostEstimate(
            flops=7 * pairs * HD, bytes_accessed=2**24, transcendentals=pairs // 2
        ),
        name="attend",
    )(slot_of, my_spans, q, d, k, v, lse, delta, base)


MESH = pl.DeviceIdType.MESH
NX = 2


def place_of():
    me = lax.axis_index("ctx")
    return me // (2 * NX), (me // 2) % NX, me % 2, lax.axis_index("head")


def device_at(z, x, core, y):
    return ((z * NX + x) * 2 + core, y)


def greet(nz, ny):
    z, x, core, y = place_of()
    barrier = pltpu.get_barrier_semaphore()

    def hello(device):
        pl.semaphore_signal(barrier, inc=1, device_id=device, device_id_type=MESH)

    for dy in range(ny):
        for dc in range(2):
            if dy or dc:
                hello(device_at(z, x, (core + dc) % 2, (y + dy) % ny))
    hello(device_at(z, 1 - x, core, y))

    @pl.when(z > 0)
    def _():
        hello(device_at(z - 1, x, core, y))

    @pl.when(z < nz - 1)
    def _():
        hello(device_at(z + 1, x, core, y))

    @pl.when((z == 0) | (z == nz - 1))
    def _():
        pl.semaphore_wait(barrier, 2 * ny + 1)

    @pl.when((z > 0) & (z < nz - 1))
    def _():
        pl.semaphore_wait(barrier, 2 * ny + 2)


def remote(src, dst, sems, index, device):
    return pltpu.make_async_remote_copy(
        src_ref=src, dst_ref=dst, send_sem=sems.at[(0, *index)], recv_sem=sems.at[(1, *index)],
        device_id=device, device_id_type=MESH,
    )


def aligned(index, size):
    return pl.ds(pl.multiple_of(index * size, size), size)


def spread_kernel(
    nz, ny, q_in, o_in, k_in, v_in, d_in, l_in, q_out, o_out, k_out, v_out, d_out, l_out,
    pair_sems, group_sems, up_sems, down_sems, side_sems,
):
    z, x, core, y = place_of()
    other = 1 - core
    own = k_in.shape[0]
    rows = 2 * own
    share = d_in.shape[0]
    sibling = device_at(z, x, other, y)
    greet(nz, ny)

    chip_row = (z * NX + x) * rows
    mine = pl.ds(pl.multiple_of(chip_row + core * own, own), own)
    pairs, keeps = [], []
    for n, (src, dst, where) in enumerate((
        (k_in, k_out, mine), (v_in, v_out, mine),
        (q_in, q_out, aligned(core, own)), (o_in, o_out, aligned(core, own)),
    )):
        width = dst.shape[1]
        pairs.append(remote(
            src.at[:, aligned(other, width)], dst.at[where, :], pair_sems, (n,), sibling
        ))
        keeps.append((dst, where, src, aligned(core, width)))
    width = d_out.shape[1]
    group = []
    d_rows = aligned(core * ny + y, share)
    for dy in range(ny):
        for dc in range(2):
            yy, cc = (y + dy) % ny, (core + dc) % 2
            columns = aligned(yy * 2 + cc, width)
            if dy or dc:
                group.append(remote(
                    d_in.at[:, columns], d_out.at[d_rows, :], group_sems, (dy, dc),
                    device_at(z, x, cc, yy),
                ))
            else:
                keeps.append((d_out, d_rows, d_in, columns))
    heads = l_out.shape[1]
    pairs.append(remote(l_in.at[aligned(other, heads), :], l_out.at[core], pair_sems, (4,), sibling))

    def keep(n):
        dst, where, src, columns = keeps[n]
        dst[where, :] = src[:, columns]

    for n in range(2):
        pairs[n].start()
        keep(n)
    for n in range(2):
        pairs[n].wait_recv()

    def hop(n, zz, sems, device):
        ref = (k_out, v_out)[n].at[aligned(zz * NX + x, rows), :]
        return remote(ref, ref, sems, (n, zz), device)

    def up(n, zz):
        return hop(n, zz, up_sems, device_at(z + 1, x, core, y))

    def down(n, zz):
        return hop(n, zz, down_sems, device_at(z - 1, x, core, y))

    def side(n, zz):
        return hop(n, zz, side_sems, device_at(z, 1 - x, core, y))

    def side_in(n, zz):
        ref = (k_out, v_out)[n].at[aligned(zz * NX + 1 - x, rows), :]
        return remote(ref, ref, side_sems, (n, zz), device_at(z, 1 - x, core, y))

    for n in range(2):
        @pl.when(z < nz - 1)
        def _():
            up(n, z).start()

        @pl.when(z > 0)
        def _():
            down(n, z).start()

        side(n, z).start()
    for copy in reversed(group):
        copy.start()
    for n in range(2, 5):
        pairs[n].start()
        keep(n)
    l_out[core] = l_in[aligned(core, heads), :]

    for step in range(1, nz):
        for n in range(2):
            @pl.when(z - step >= 0)
            def _():
                up(n, z - step).wait_recv()

                @pl.when(z < nz - 1)
                def _():
                    up(n, z - step).start()

                side(n, z - step).start()

            @pl.when(z + step < nz)
            def _():
                down(n, z + step).wait_recv()

                @pl.when(z > 0)
                def _():
                    down(n, z + step).start()

                side(n, z + step).start()

    for n in range(2):
        for zz in range(nz):
            side_in(n, zz).wait_recv()
            side(n, zz).wait_send()

            @pl.when((zz <= z) & (z < nz - 1))
            def _():
                up(n, zz).wait_send()

            @pl.when((zz >= z) & (z > 0))
            def _():
                down(n, zz).wait_send()

        pairs[n].wait_send()
        pairs[n + 2].wait()
    pairs[4].wait()
    for copy in group:
        copy.wait()


def spread(q, o, k, v, d, lse, ctx, ny):
    nz = ctx // (2 * NX)
    rows = 2 * q.shape[0]
    seq = k.shape[0] * ctx

    def like(height, x, parts):
        return jax.ShapeDtypeStruct((height, x.shape[1] // parts), x.dtype)

    whole = pl.BlockSpec(memory_space=pltpu.VMEM)
    dma = pltpu.SemaphoreType.DMA
    return pl.pallas_call(
        functools.partial(spread_kernel, nz, ny),
        out_shape=[like(rows, q, 2), like(rows, o, 2), like(seq, k, 2), like(seq, v, 2),
                   like(rows, d, 2 * ny),
                   jax.ShapeDtypeStruct((2, lse.shape[0] // 2, lse.shape[1]), lse.dtype)],
        in_specs=[whole] * 6,
        out_specs=[whole] * 6,
        scratch_shapes=[
            dma((2, 5)), dma((2, ny, 2)), dma((2, 2, nz)), dma((2, 2, nz)), dma((2, 2, nz)),
        ],
        compiler_params=pltpu.CompilerParams(
            collective_id=0, has_side_effects=True, vmem_limit_bytes=40 * 2**20
        ),
        name="spread",
    )(q, o, k, v, d, lse)


def fold_kernel(
    nz, ny, dk_in, dv_in, dq_in, gk_out, gv_out, gq_out,
    side_buf, up_buf, down_buf, out_buf, fin,
    local_sems, pair_sems, group_sems, up_sems, down_sems, side_sems,
):
    z, x, core, y = place_of()
    other = 1 - core
    rows = fin.shape[1]
    own = rows // 2
    share = gq_out.shape[0]
    parts = (dk_in, dv_in)
    greet(nz, ny)

    def side(n, zz):
        return remote(
            parts[n].at[aligned(zz * NX + 1 - x, rows), :], side_buf.at[n, zz], side_sems, (n, zz),
            device_at(z, 1 - x, core, y),
        )

    def up(n, zz):
        return remote(
            out_buf.at[n, zz], up_buf.at[n, zz], up_sems, (n, zz), device_at(z + 1, x, core, y)
        )

    def down(n, zz):
        return remote(
            out_buf.at[n, zz], down_buf.at[n, zz], down_sems, (n, zz), device_at(z - 1, x, core, y)
        )

    order = []
    for far in range(nz // 2):
        order.append(jnp.where(z < nz // 2, nz - 1 - far, far))
        order.append(jnp.where(z < nz // 2, far, nz - 1 - far))

    width = dq_in.shape[1]
    group = []
    for dy in range(ny):
        for dc in range(2):
            yy, cc = (y + dy) % ny, (core + dc) % 2
            src = dq_in.at[aligned(cc * ny + yy, share), :]
            dst = gq_out.at[:, aligned(y * 2 + core, width)]
            if dy or dc:
                group.append(remote(src, dst, group_sems, (dy, dc), device_at(z, x, cc, yy)))
            else:
                keep = pltpu.make_async_copy(src, dst, local_sems.at[2])
    for zz in order:
        for n in range(2):
            side(n, zz).start()
    for copy in reversed(group):
        copy.start()
    keep.start()

    def total(n, zz):
        mine = parts[n][aligned(zz * NX + x, rows), :].astype(jnp.float32)
        return mine + side_buf[n, zz].astype(jnp.float32)

    for zz in order:
        for n in range(2):
            @pl.when(zz > z)
            def _():
                side(n, zz).wait_recv()

                @pl.when(z == 0)
                def _():
                    out_buf[n, zz] = total(n, zz).astype(jnp.bfloat16)

                @pl.when(z > 0)
                def _():
                    up(n, zz).wait_recv()
                    out_buf[n, zz] = (
                        total(n, zz) + up_buf[n, zz].astype(jnp.float32)
                    ).astype(jnp.bfloat16)

                up(n, zz).start()

            @pl.when(zz < z)
            def _():
                side(n, zz).wait_recv()

                @pl.when(z == nz - 1)
                def _():
                    out_buf[n, zz] = total(n, zz).astype(jnp.bfloat16)

                @pl.when(z < nz - 1)
                def _():
                    down(n, zz).wait_recv()
                    out_buf[n, zz] = (
                        total(n, zz) + down_buf[n, zz].astype(jnp.float32)
                    ).astype(jnp.bfloat16)

                down(n, zz).start()

    ends = []
    for n, out in enumerate((gk_out, gv_out)):
        side(n, z).wait_recv()

        @pl.when(z == 0)
        def _():
            down(n, z).wait_recv()
            fin[n] = (total(n, z) + down_buf[n, z].astype(jnp.float32)).astype(jnp.bfloat16)

        @pl.when(z == nz - 1)
        def _():
            up(n, z).wait_recv()
            fin[n] = (total(n, z) + up_buf[n, z].astype(jnp.float32)).astype(jnp.bfloat16)

        @pl.when((z > 0) & (z < nz - 1))
        def _():
            up(n, z).wait_recv()
            down(n, z).wait_recv()
            fin[n] = (
                total(n, z) + up_buf[n, z].astype(jnp.float32) + down_buf[n, z].astype(jnp.float32)
            ).astype(jnp.bfloat16)

        columns = aligned(core, fin.shape[2])
        pair = remote(
            fin.at[n, aligned(other, own), :], out.at[:, columns], pair_sems, (n,),
            device_at(z, x, other, y),
        )
        here = pltpu.make_async_copy(
            fin.at[n, aligned(core, own), :], out.at[:, columns], local_sems.at[n]
        )
        pair.start()
        here.start()
        ends += [pair, here]

    for copy in ends + group + [keep]:
        copy.wait()
    for n in range(2):
        for zz in range(nz):
            side(n, zz).wait_send()

            @pl.when(zz > z)
            def _():
                up(n, zz).wait_send()

            @pl.when(zz < z)
            def _():
                down(n, zz).wait_send()


def fold(dk, dv, dq, ctx, ny):
    nz = ctx // (2 * NX)
    rows = dq.shape[0]
    own = rows // 2
    width = dk.shape[1]
    anywhere = pl.BlockSpec(memory_space=pl.ANY)
    whole = pl.BlockSpec(memory_space=pltpu.VMEM)
    dma = pltpu.SemaphoreType.DMA
    buffers = pltpu.VMEM((2, nz, rows, width), jnp.bfloat16)
    kv_out = jax.ShapeDtypeStruct((own, 2 * width), jnp.bfloat16)
    return pl.pallas_call(
        functools.partial(fold_kernel, nz, ny),
        out_shape=[kv_out, kv_out,
                   jax.ShapeDtypeStruct((rows // (2 * ny), dq.shape[1] * 2 * ny), jnp.bfloat16)],
        in_specs=[whole, whole, anywhere],
        out_specs=[anywhere] * 3,
        scratch_shapes=[
            buffers, buffers, buffers, buffers, pltpu.VMEM((2, rows, width), jnp.bfloat16),
            dma((3,)), dma((2, 2)), dma((2, ny, 2)), dma((2, 2, nz)), dma((2, 2, nz)), dma((2, 2, nz)),
        ],
        compiler_params=pltpu.CompilerParams(
            collective_id=1, has_side_effects=True, vmem_limit_bytes=32 * 2**20
        ),
        name="fold",
    )(dk, dv, dq)


def row_terms_of(terms, kv_heads, span):
    rows = terms.shape[1]
    cut = terms.reshape(kv_heads, GROUPS, rows // span, span)
    return cut.transpose(0, 2, 1, 3).reshape(kv_heads, rows // span, 1, GROUPS * span)


def per_device(query_rows, key_rows, value_rows, attn_output, log_norms, grad_output, span_order):
    own_rows = query_rows.shape[0]
    span = own_rows // 2
    ctx = lax.axis_size("ctx")
    me = lax.axis_index("ctx")
    cores = 2 if (key_rows.shape[1] // HD) % 2 == 0 and ctx % 2 == 0 else 1
    chip_groups = [[i * cores + c for c in range(cores)] for i in range(ctx // cores)]
    ring_groups = [[i * cores + c for i in range(ctx // cores)] for c in range(cores)]

    def to_heads(x, split=1, concat=0):
        if cores == 1:
            return x
        return lax.all_to_all(
            x, "ctx", split_axis=split, concat_axis=concat, axis_index_groups=chip_groups, tiled=True
        )

    ny = lax.axis_size("head")
    by_kernels = cores == 2 and ctx % (4 * NX) == 0
    if by_kernels:
        q, o, k, v, d, lse = spread(
            query_rows, attn_output, key_rows, value_rows, grad_output, log_norms, ctx, ny
        )
        lse = jnp.concatenate([lse[0], lse[1]], axis=1)
    else:
        lse = to_heads(log_norms, 0, 1)
        q = to_heads(query_rows)
        o = to_heads(attn_output)
        d = to_heads(lax.all_to_all(grad_output, "head", split_axis=1, concat_axis=0, tiled=True))
        kv = jnp.concatenate([to_heads(key_rows), to_heads(value_rows)], axis=1)
        kv = lax.all_gather(kv, "ctx", axis=0, axis_index_groups=ring_groups, tiled=True)
        k, v = kv[:, :kv.shape[1] // 2], kv[:, kv.shape[1] // 2:]
    half = k.shape[1]
    kv_heads = half // HD
    rows = q.shape[0]
    delta = jnp.sum(
        (d.astype(jnp.float32) * o.astype(jnp.float32)).reshape(rows, kv_heads * GROUPS, HD), axis=-1
    ).T
    spans = span_order.shape[0]
    slots = rows // span
    ids = jnp.arange(spans, dtype=jnp.int32)
    slot_of = jnp.sum(jnp.where(span_order[None, :] == ids[:, None], ids[None, :], 0), axis=1)
    my_spans = lax.dynamic_slice_in_dim(span_order, (me // cores) * slots, slots)
    dq, dk, dv = attend(
        slot_of, my_spans, q, d, k, v,
        row_terms_of(lse * LOG2E, kv_heads, span), row_terms_of(delta, kv_heads, span),
        span, jnp.bfloat16 if by_kernels else jnp.float32,
    )
    if by_kernels:
        grad_key, grad_value, grad_query = fold(dk, dv, dq, ctx, ny)
        return (grad_query, grad_key, grad_value)
    dkv = jnp.concatenate([dk, dv], axis=1)
    dkv = lax.psum_scatter(dkv, "ctx", scatter_dimension=0, axis_index_groups=ring_groups, tiled=True)
    dkv = dkv.astype(jnp.bfloat16)
    grad_key = to_heads(dkv[:, :half], 0, 1)
    grad_value = to_heads(dkv[:, half:], 0, 1)
    dq = to_heads(dq, 0, 1)
    grad_query = lax.all_to_all(dq, "head", split_axis=0, concat_axis=1, tiled=True)
    return (grad_query, grad_key, grad_value)


def solution(mesh):
    return jax.shard_map(
        per_device,
        mesh=mesh,
        in_specs=(
            P("ctx", "head"),
            P("ctx", "head"),
            P("ctx", "head"),
            P("ctx", "head"),
            P("head", "ctx"),
            P(("ctx", "head"), None),
            P(),
        ),
        out_specs=(P(("ctx", "head"), None), P("ctx", "head"), P("ctx", "head")),
        check_vma=False,
    )
```

```python
import functools
import math

import jax
import jax.numpy as jnp
from jax import lax
from jax.experimental import pallas as pl
from jax.experimental.pallas import tpu as pltpu
from jax.sharding import PartitionSpec as P

QH = 64
KVH = 8
HD = 128
GROUPS = QH // KVH
KEYS = 256
LOG2E = math.log2(math.e)


def over_rows(left, right):
    return lax.dot_general(
        left, right, (((1,), (1,)), ((), ())), preferred_element_type=jnp.float32
    )


def attend_kernel(
    slot_of_ref, my_span_ref,
    q_ref, d_ref, k_ref, v_ref, lse_ref, delta_ref, base_ref,
    dq_ref, dk_ref, dv_ref,
    ks, kt, vs, qs, qt, ds_rows, dt, dqt, dk_acc, dv_acc,
):
    span = base_ref.shape[1] // GROUPS
    seq = k_ref.shape[0]
    slots = q_ref.shape[0] // span
    inv_root = HD ** -0.5

    def place(p, _):
        src = pl.ds(pl.multiple_of(slot_of_ref[p] * span, span), span)
        dst = pl.ds(pl.multiple_of(p * span, span), span)
        ks[dst, :] = k_ref[src, :]
        vs[dst, :] = v_ref[src, :]
        return 0

    lax.fori_loop(0, seq // span, place, 0)

    def turn(c, _):
        rows = pl.ds(pl.multiple_of(c * KEYS, KEYS), KEYS)
        kt[c] = ks[rows, :].T
        dk_acc[c] = jnp.zeros((HD, KEYS), jnp.float32)
        dv_acc[c] = jnp.zeros((HD, KEYS), jnp.float32)
        return 0

    lax.fori_loop(0, seq // KEYS, turn, 0)

    def one_slot(s, _):
        rows = pl.ds(pl.multiple_of(s * span, span), span)
        for g in range(GROUPS):
            part = slice(g * span, (g + 1) * span)
            cols = slice(g * HD, (g + 1) * HD)
            qs[part, :] = q_ref[rows, cols]
            ds_rows[part, :] = d_ref[rows, cols]
        qt[...] = qs[...].T
        dt[...] = ds_rows[...].T
        dqt[...] = jnp.zeros_like(dqt)
        my_span = my_span_ref[s]

        def block(c, masked, size=1):
            wide = qt.shape[1]
            cuts = [slice(j, min(j + KEYS, wide)) for j in range(0, wide, KEYS)]
            tiles = [(i, cut) for i in range(size) for cut in cuts]

            def keys_of(i):
                return pl.ds(pl.multiple_of((c + i) * KEYS, KEYS), KEYS)

            def products(i, cut):
                scores = jnp.dot(ks[keys_of(i), :], qt[:, cut], preferred_element_type=jnp.float32)
                dprob = jnp.dot(vs[keys_of(i), :], dt[:, cut], preferred_element_type=jnp.float32)
                return scores, dprob

            probs, dscores = [], []
            ahead = products(*tiles[0])
            for n, (i, cut) in enumerate(tiles):
                scores, dprob = ahead
                if n + 1 < len(tiles):
                    ahead = products(*tiles[n + 1])
                prob = jnp.exp2(scores * (inv_root * LOG2E) - lse_ref[0, s][:, cut])
                if masked:
                    key_pos = (c + i) * KEYS + lax.broadcasted_iota(jnp.int32, prob.shape, 0)
                    prob = jnp.where(my_span * span + base_ref[:, cut] >= key_pos, prob, 0.0)
                dscores.append((prob * (dprob - delta_ref[0, s][:, cut])).astype(jnp.bfloat16))
                probs.append(prob.astype(jnp.bfloat16))
                if cut is cuts[-1]:
                    prob_low = jnp.concatenate(probs[-len(cuts):], axis=1)
                    dscore = jnp.concatenate(dscores[-len(cuts):], axis=1)
                    dv_acc[c + i] += over_rows(dt[...], prob_low)
                    dk_acc[c + i] += over_rows(qt[...], dscore)
                    dqt[...] += jnp.dot(kt[c + i], dscore, preferred_element_type=jnp.float32)

        whole = (my_span * span) // KEYS
        last = (my_span * span + span + KEYS - 1) // KEYS
        lax.fori_loop(0, whole // 2, lambda c, _: (block(2 * c, False, 2), 0)[1], 0)

        @pl.when(whole % 2 == 1)
        def _():
            block(whole - 1, False)

        lax.fori_loop(whole, last, lambda c, _: (block(c, True), 0)[1], 0)

        dq = (dqt[...].T * inv_root).astype(jnp.bfloat16)
        for g in range(GROUPS):
            dq_ref[rows, g * HD:(g + 1) * HD] = dq[g * span:(g + 1) * span, :]
        return 0

    lax.fori_loop(0, slots, one_slot, 0)

    def straighten(c, _):
        rows = pl.ds(pl.multiple_of(c * KEYS, KEYS), KEYS)
        ks[rows, :] = (dk_acc[c].T * inv_root).astype(ks.dtype)
        vs[rows, :] = dv_acc[c].T.astype(vs.dtype)
        return 0

    lax.fori_loop(0, seq // KEYS, straighten, 0)

    def back(p, _):
        dst = pl.ds(pl.multiple_of(slot_of_ref[p] * span, span), span)
        src = pl.ds(pl.multiple_of(p * span, span), span)
        dk_ref[dst, :] = ks[src, :].astype(dk_ref.dtype)
        dv_ref[dst, :] = vs[src, :].astype(dv_ref.dtype)
        return 0

    lax.fori_loop(0, seq // span, back, 0)


def attend(slot_of, my_spans, q, d, k, v, lse, delta, span, part_type):
    rows = q.shape[0]
    seq = k.shape[0]
    kv_heads = k.shape[1] // HD
    slots = rows // span
    wide = GROUPS * span
    base = jnp.tile(jnp.arange(span, dtype=jnp.int32), GROUPS)[None, :]
    pairs = kv_heads * wide * seq * slots

    def by_head(height, width):
        return pl.BlockSpec((height, width), lambda h, *_: (0, h))

    row_terms = pl.BlockSpec((1, slots, 1, wide), lambda h, *_: (h, 0, 0, 0))
    return pl.pallas_call(
        attend_kernel,
        grid_spec=pltpu.PrefetchScalarGridSpec(
            num_scalar_prefetch=2,
            grid=(kv_heads,),
            in_specs=[
                by_head(rows, GROUPS * HD), by_head(rows, GROUPS * HD),
                by_head(seq, HD), by_head(seq, HD),
                row_terms, row_terms,
                pl.BlockSpec((1, wide), lambda h, *_: (0, 0)),
            ],
            out_specs=[by_head(rows, GROUPS * HD), by_head(seq, HD), by_head(seq, HD)],
            scratch_shapes=[
                pltpu.VMEM((seq, HD), jnp.bfloat16),
                pltpu.VMEM((seq // KEYS, HD, KEYS), jnp.bfloat16),
                pltpu.VMEM((seq, HD), jnp.bfloat16),
                pltpu.VMEM((wide, HD), jnp.bfloat16),
                pltpu.VMEM((HD, wide), jnp.bfloat16),
                pltpu.VMEM((wide, HD), jnp.bfloat16),
                pltpu.VMEM((HD, wide), jnp.bfloat16),
                pltpu.VMEM((HD, wide), jnp.float32),
                pltpu.VMEM((seq // KEYS, HD, KEYS), jnp.float32),
                pltpu.VMEM((seq // KEYS, HD, KEYS), jnp.float32),
            ],
        ),
        out_shape=[
            jax.ShapeDtypeStruct(q.shape, jnp.bfloat16),
            jax.ShapeDtypeStruct(k.shape, part_type),
            jax.ShapeDtypeStruct(k.shape, part_type),
        ],
        compiler_params=pltpu.CompilerParams(vmem_limit_bytes=48 * 2**20),
        cost_estimate=pl.CostEstimate(
            flops=7 * pairs * HD, bytes_accessed=2**24, transcendentals=pairs // 2
        ),
        name="attend",
    )(slot_of, my_spans, q, d, k, v, lse, delta, base)


MESH = pl.DeviceIdType.MESH
NX = 2


def place_of():
    me = lax.axis_index("ctx")
    return me // (2 * NX), (me // 2) % NX, me % 2, lax.axis_index("head")


def device_at(z, x, core, y):
    return ((z * NX + x) * 2 + core, y)


def greet(nz, ny):
    z, x, core, y = place_of()
    barrier = pltpu.get_barrier_semaphore()

    def hello(device):
        pl.semaphore_signal(barrier, inc=1, device_id=device, device_id_type=MESH)

    for dy in range(ny):
        for dc in range(2):
            if dy or dc:
                hello(device_at(z, x, (core + dc) % 2, (y + dy) % ny))
    hello(device_at(z, 1 - x, core, y))

    @pl.when(z > 0)
    def _():
        hello(device_at(z - 1, x, core, y))

    @pl.when(z < nz - 1)
    def _():
        hello(device_at(z + 1, x, core, y))

    @pl.when((z == 0) | (z == nz - 1))
    def _():
        pl.semaphore_wait(barrier, 2 * ny + 1)

    @pl.when((z > 0) & (z < nz - 1))
    def _():
        pl.semaphore_wait(barrier, 2 * ny + 2)


def remote(src, dst, sems, index, device):
    return pltpu.make_async_remote_copy(
        src_ref=src, dst_ref=dst, send_sem=sems.at[(0, *index)], recv_sem=sems.at[(1, *index)],
        device_id=device, device_id_type=MESH,
    )


def aligned(index, size):
    return pl.ds(pl.multiple_of(index * size, size), size)


def spread_kernel(
    nz, ny, q_hbm, o_hbm, k_in, v_in, d_hbm, l_in, q_hbm_out, d_hbm_out, k_out, v_out, l_out, delta_out,
    q_in, o_in, d_in, q_out, o_out, d_out, local_sems,
    pair_sems, group_sems, up_sems, down_sems, side_sems,
):
    z, x, core, y = place_of()
    other = 1 - core
    own = k_in.shape[0]
    rows = 2 * own
    share = d_in.shape[0]
    sibling = device_at(z, x, other, y)
    staged = [
        pltpu.make_async_copy(src, dst, local_sems.at[n])
        for n, (src, dst) in enumerate(((d_hbm, d_in), (q_hbm, q_in), (o_hbm, o_in)))
    ]
    flushed = [
        pltpu.make_async_copy(src, dst, local_sems.at[3 + n])
        for n, (src, dst) in enumerate(((d_out, d_hbm_out), (q_out, q_hbm_out)))
    ]
    for copy in staged:
        copy.start()
    greet(nz, ny)

    chip_row = (z * NX + x) * rows
    mine = pl.ds(pl.multiple_of(chip_row + core * own, own), own)
    pairs, keeps = [], []
    for n, (src, dst, where) in enumerate((
        (k_in, k_out, mine), (v_in, v_out, mine),
        (q_in, q_out, aligned(core, own)), (o_in, o_out, aligned(core, own)),
    )):
        width = dst.shape[1]
        pairs.append(remote(
            src.at[:, aligned(other, width)], dst.at[where, :], pair_sems, (n,), sibling
        ))
        keeps.append((dst, where, src, aligned(core, width)))
    width = d_out.shape[1]
    group = []
    d_rows = aligned(core * ny + y, share)
    for dy in range(ny):
        for dc in range(2):
            yy, cc = (y + dy) % ny, (core + dc) % 2
            columns = aligned(yy * 2 + cc, width)
            if dy or dc:
                group.append(remote(
                    d_in.at[:, columns], d_out.at[d_rows, :], group_sems, (dy, dc),
                    device_at(z, x, cc, yy),
                ))
            else:
                keeps.append((d_out, d_rows, d_in, columns))
    heads = l_out.shape[1]
    pairs.append(remote(l_in.at[aligned(other, heads), :], l_out.at[core], pair_sems, (4,), sibling))

    def keep(n):
        dst, where, src, columns = keeps[n]
        dst[where, :] = src[:, columns]

    for n in range(2):
        pairs[n].start()
        keep(n)
    for n in range(2):
        pairs[n].wait_recv()

    def hop(n, zz, sems, device):
        ref = (k_out, v_out)[n].at[aligned(zz * NX + x, rows), :]
        return remote(ref, ref, sems, (n, zz), device)

    def up(n, zz):
        return hop(n, zz, up_sems, device_at(z + 1, x, core, y))

    def down(n, zz):
        return hop(n, zz, down_sems, device_at(z - 1, x, core, y))

    def side(n, zz):
        return hop(n, zz, side_sems, device_at(z, 1 - x, core, y))

    def side_in(n, zz):
        ref = (k_out, v_out)[n].at[aligned(zz * NX + 1 - x, rows), :]
        return remote(ref, ref, side_sems, (n, zz), device_at(z, 1 - x, core, y))

    for n in range(2):
        @pl.when(z < nz - 1)
        def _():
            up(n, z).start()

        @pl.when(z > 0)
        def _():
            down(n, z).start()

        side(n, z).start()
    staged[0].wait()
    for copy in reversed(group):
        copy.start()
    staged[1].wait()
    staged[2].wait()
    for n in range(2, 5):
        pairs[n].start()
        keep(n)
    l_out[core] = l_in[aligned(core, heads), :]

    for step in range(1, nz):
        for n in range(2):
            @pl.when(z - step >= 0)
            def _():
                up(n, z - step).wait_recv()

                @pl.when(z < nz - 1)
                def _():
                    up(n, z - step).start()

                side(n, z - step).start()

            @pl.when(z + step < nz)
            def _():
                down(n, z + step).wait_recv()

                @pl.when(z > 0)
                def _():
                    down(n, z + step).start()

                side(n, z + step).start()

    for copy in group + pairs[2:]:
        copy.wait()
    for copy in flushed:
        copy.start()
    for h in range(delta_out.shape[0]):
        cols = slice(h * HD, (h + 1) * HD)
        terms = d_out[:, cols].astype(jnp.float32) * o_out[:, cols].astype(jnp.float32)
        delta_out[h:h + 1, :] = jnp.sum(terms.T, axis=0, keepdims=True)

    for n in range(2):
        for zz in range(nz):
            side_in(n, zz).wait_recv()
            side(n, zz).wait_send()

            @pl.when((zz <= z) & (z < nz - 1))
            def _():
                up(n, zz).wait_send()

            @pl.when((zz >= z) & (z > 0))
            def _():
                down(n, zz).wait_send()

        pairs[n].wait_send()
    for copy in flushed:
        copy.wait()


def spread(q, o, k, v, d, lse, ctx, ny):
    nz = ctx // (2 * NX)
    rows = 2 * q.shape[0]
    seq = k.shape[0] * ctx

    def like(height, x, parts):
        return jax.ShapeDtypeStruct((height, x.shape[1] // parts), x.dtype)

    anywhere = pl.BlockSpec(memory_space=pl.ANY)
    whole = pl.BlockSpec(memory_space=pltpu.VMEM)
    dma = pltpu.SemaphoreType.DMA
    return pl.pallas_call(
        functools.partial(spread_kernel, nz, ny),
        out_shape=[like(rows, q, 2), like(rows, d, 2 * ny), like(seq, k, 2), like(seq, v, 2),
                   jax.ShapeDtypeStruct((2, lse.shape[0] // 2, lse.shape[1]), lse.dtype),
                   jax.ShapeDtypeStruct((lse.shape[0] // 2, rows), jnp.float32)],
        in_specs=[anywhere, anywhere, whole, whole, anywhere, whole],
        out_specs=[anywhere, anywhere, whole, whole, whole, whole],
        scratch_shapes=[
            pltpu.VMEM(q.shape, q.dtype), pltpu.VMEM(o.shape, o.dtype), pltpu.VMEM(d.shape, d.dtype),
            pltpu.VMEM((rows, q.shape[1] // 2), q.dtype), pltpu.VMEM((rows, q.shape[1] // 2), o.dtype),
            pltpu.VMEM((rows, q.shape[1] // 2), d.dtype), dma((5,)),
            dma((2, 5)), dma((2, ny, 2)), dma((2, 2, nz)), dma((2, 2, nz)), dma((2, 2, nz)),
        ],
        compiler_params=pltpu.CompilerParams(
            collective_id=0, has_side_effects=True, vmem_limit_bytes=40 * 2**20
        ),
        name="spread",
    )(q, o, k, v, d, lse)


def fold_kernel(
    nz, ny, dk_in, dv_in, dq_in, gk_out, gv_out, gq_out,
    side_buf, up_buf, down_buf, out_buf, fin,
    local_sems, pair_sems, group_sems, up_sems, down_sems, side_sems,
):
    z, x, core, y = place_of()
    other = 1 - core
    rows = fin.shape[1]
    own = rows // 2
    share = gq_out.shape[0]
    parts = (dk_in, dv_in)
    greet(nz, ny)

    def side(n, zz):
        return remote(
            parts[n].at[aligned(zz * NX + 1 - x, rows), :], side_buf.at[n, zz], side_sems, (n, zz),
            device_at(z, 1 - x, core, y),
        )

    def up(n, zz):
        return remote(
            out_buf.at[n, zz], up_buf.at[n, zz], up_sems, (n, zz), device_at(z + 1, x, core, y)
        )

    def down(n, zz):
        return remote(
            out_buf.at[n, zz], down_buf.at[n, zz], down_sems, (n, zz), device_at(z - 1, x, core, y)
        )

    order = []
    for far in range(nz // 2):
        order.append(jnp.where(z < nz // 2, nz - 1 - far, far))
        order.append(jnp.where(z < nz // 2, far, nz - 1 - far))

    width = dq_in.shape[1]
    group = []
    for dy in range(ny):
        for dc in range(2):
            yy, cc = (y + dy) % ny, (core + dc) % 2
            src = dq_in.at[aligned(cc * ny + yy, share), :]
            dst = gq_out.at[:, aligned(y * 2 + core, width)]
            if dy or dc:
                group.append(remote(src, dst, group_sems, (dy, dc), device_at(z, x, cc, yy)))
            else:
                keep = pltpu.make_async_copy(src, dst, local_sems.at[2])
    for zz in order:
        for n in range(2):
            side(n, zz).start()
    for copy in reversed(group):
        copy.start()
    keep.start()

    def total(n, zz):
        mine = parts[n][aligned(zz * NX + x, rows), :].astype(jnp.float32)
        return mine + side_buf[n, zz].astype(jnp.float32)

    for zz in order:
        for n in range(2):
            @pl.when(zz > z)
            def _():
                side(n, zz).wait_recv()

                @pl.when(z == 0)
                def _():
                    out_buf[n, zz] = total(n, zz).astype(jnp.bfloat16)

                @pl.when(z > 0)
                def _():
                    up(n, zz).wait_recv()
                    out_buf[n, zz] = (
                        total(n, zz) + up_buf[n, zz].astype(jnp.float32)
                    ).astype(jnp.bfloat16)

                up(n, zz).start()

            @pl.when(zz < z)
            def _():
                side(n, zz).wait_recv()

                @pl.when(z == nz - 1)
                def _():
                    out_buf[n, zz] = total(n, zz).astype(jnp.bfloat16)

                @pl.when(z < nz - 1)
                def _():
                    down(n, zz).wait_recv()
                    out_buf[n, zz] = (
                        total(n, zz) + down_buf[n, zz].astype(jnp.float32)
                    ).astype(jnp.bfloat16)

                down(n, zz).start()

    ends = []
    for n, out in enumerate((gk_out, gv_out)):
        side(n, z).wait_recv()

        @pl.when(z == 0)
        def _():
            down(n, z).wait_recv()
            fin[n] = (total(n, z) + down_buf[n, z].astype(jnp.float32)).astype(jnp.bfloat16)

        @pl.when(z == nz - 1)
        def _():
            up(n, z).wait_recv()
            fin[n] = (total(n, z) + up_buf[n, z].astype(jnp.float32)).astype(jnp.bfloat16)

        @pl.when((z > 0) & (z < nz - 1))
        def _():
            up(n, z).wait_recv()
            down(n, z).wait_recv()
            fin[n] = (
                total(n, z) + up_buf[n, z].astype(jnp.float32) + down_buf[n, z].astype(jnp.float32)
            ).astype(jnp.bfloat16)

        columns = aligned(core, fin.shape[2])
        pair = remote(
            fin.at[n, aligned(other, own), :], out.at[:, columns], pair_sems, (n,),
            device_at(z, x, other, y),
        )
        here = pltpu.make_async_copy(
            fin.at[n, aligned(core, own), :], out.at[:, columns], local_sems.at[n]
        )
        pair.start()
        here.start()
        ends += [pair, here]

    for copy in ends + group + [keep]:
        copy.wait()
    for n in range(2):
        for zz in range(nz):
            side(n, zz).wait_send()

            @pl.when(zz > z)
            def _():
                up(n, zz).wait_send()

            @pl.when(zz < z)
            def _():
                down(n, zz).wait_send()


def fold(dk, dv, dq, ctx, ny):
    nz = ctx // (2 * NX)
    rows = dq.shape[0]
    own = rows // 2
    width = dk.shape[1]
    anywhere = pl.BlockSpec(memory_space=pl.ANY)
    whole = pl.BlockSpec(memory_space=pltpu.VMEM)
    dma = pltpu.SemaphoreType.DMA
    buffers = pltpu.VMEM((2, nz, rows, width), jnp.bfloat16)
    kv_out = jax.ShapeDtypeStruct((own, 2 * width), jnp.bfloat16)
    return pl.pallas_call(
        functools.partial(fold_kernel, nz, ny),
        out_shape=[kv_out, kv_out,
                   jax.ShapeDtypeStruct((rows // (2 * ny), dq.shape[1] * 2 * ny), jnp.bfloat16)],
        in_specs=[whole, whole, anywhere],
        out_specs=[anywhere] * 3,
        scratch_shapes=[
            buffers, buffers, buffers, buffers, pltpu.VMEM((2, rows, width), jnp.bfloat16),
            dma((3,)), dma((2, 2)), dma((2, ny, 2)), dma((2, 2, nz)), dma((2, 2, nz)), dma((2, 2, nz)),
        ],
        compiler_params=pltpu.CompilerParams(
            collective_id=1, has_side_effects=True, vmem_limit_bytes=32 * 2**20
        ),
        name="fold",
    )(dk, dv, dq)


def row_terms_of(terms, kv_heads, span):
    rows = terms.shape[1]
    cut = terms.reshape(kv_heads, GROUPS, rows // span, span)
    return cut.transpose(0, 2, 1, 3).reshape(kv_heads, rows // span, 1, GROUPS * span)


def per_device(query_rows, key_rows, value_rows, attn_output, log_norms, grad_output, span_order):
    own_rows = query_rows.shape[0]
    span = own_rows // 2
    ctx = lax.axis_size("ctx")
    me = lax.axis_index("ctx")
    cores = 2 if (key_rows.shape[1] // HD) % 2 == 0 and ctx % 2 == 0 else 1
    chip_groups = [[i * cores + c for c in range(cores)] for i in range(ctx // cores)]
    ring_groups = [[i * cores + c for i in range(ctx // cores)] for c in range(cores)]

    def to_heads(x, split=1, concat=0):
        if cores == 1:
            return x
        return lax.all_to_all(
            x, "ctx", split_axis=split, concat_axis=concat, axis_index_groups=chip_groups, tiled=True
        )

    ny = lax.axis_size("head")
    by_kernels = cores == 2 and ctx % (4 * NX) == 0
    if by_kernels:
        q, d, k, v, lse, delta = spread(
            query_rows, attn_output, key_rows, value_rows, grad_output, log_norms, ctx, ny
        )
        lse = jnp.concatenate([lse[0], lse[1]], axis=1)
    else:
        lse = to_heads(log_norms, 0, 1)
        q = to_heads(query_rows)
        o = to_heads(attn_output)
        d = to_heads(lax.all_to_all(grad_output, "head", split_axis=1, concat_axis=0, tiled=True))
        kv = jnp.concatenate([to_heads(key_rows), to_heads(value_rows)], axis=1)
        kv = lax.all_gather(kv, "ctx", axis=0, axis_index_groups=ring_groups, tiled=True)
        k, v = kv[:, :kv.shape[1] // 2], kv[:, kv.shape[1] // 2:]
    half = k.shape[1]
    kv_heads = half // HD
    rows = q.shape[0]
    if not by_kernels:
        terms = d.astype(jnp.float32) * o.astype(jnp.float32)
        delta = jnp.sum(terms.reshape(rows, kv_heads * GROUPS, HD), axis=-1).T
    spans = span_order.shape[0]
    slots = rows // span
    ids = jnp.arange(spans, dtype=jnp.int32)
    slot_of = jnp.sum(jnp.where(span_order[None, :] == ids[:, None], ids[None, :], 0), axis=1)
    my_spans = lax.dynamic_slice_in_dim(span_order, (me // cores) * slots, slots)
    dq, dk, dv = attend(
        slot_of, my_spans, q, d, k, v,
        row_terms_of(lse * LOG2E, kv_heads, span), row_terms_of(delta, kv_heads, span),
        span, jnp.bfloat16 if by_kernels else jnp.float32,
    )
    if by_kernels:
        grad_key, grad_value, grad_query = fold(dk, dv, dq, ctx, ny)
        return (grad_query, grad_key, grad_value)
    dkv = jnp.concatenate([dk, dv], axis=1)
    dkv = lax.psum_scatter(dkv, "ctx", scatter_dimension=0, axis_index_groups=ring_groups, tiled=True)
    dkv = dkv.astype(jnp.bfloat16)
    grad_key = to_heads(dkv[:, :half], 0, 1)
    grad_value = to_heads(dkv[:, half:], 0, 1)
    dq = to_heads(dq, 0, 1)
    grad_query = lax.all_to_all(dq, "head", split_axis=0, concat_axis=1, tiled=True)
    return (grad_query, grad_key, grad_value)


def solution(mesh):
    return jax.shard_map(
        per_device,
        mesh=mesh,
        in_specs=(
            P("ctx", "head"),
            P("ctx", "head"),
            P("ctx", "head"),
            P("ctx", "head"),
            P("head", "ctx"),
            P(("ctx", "head"), None),
            P(),
        ),
        out_specs=(P(("ctx", "head"), None), P("ctx", "head"), P("ctx", "head")),
        check_vma=False,
    )
```

```python
import functools
import math

import jax
import jax.numpy as jnp
from jax import lax
from jax.experimental import pallas as pl
from jax.experimental.pallas import tpu as pltpu
from jax.sharding import PartitionSpec as P

QH = 64
KVH = 8
HD = 128
GROUPS = QH // KVH
KEYS = 256
LOG2E = math.log2(math.e)


def attend_kernel(
    slot_of_ref, my_span_ref,
    q_ref, d_ref, k_ref, v_ref, lse_ref, delta_ref, base_ref,
    dq_ref, dk_ref, dv_ref,
    ks, kt, vs, qs, qt, ds_rows, dt, dqt, dk_acc, dv_acc,
):
    span = base_ref.shape[1] // GROUPS
    seq = k_ref.shape[0]
    slots = q_ref.shape[0] // span
    inv_root = HD ** -0.5

    def place(p, _):
        src = pl.ds(pl.multiple_of(slot_of_ref[p] * span, span), span)
        dst = pl.ds(pl.multiple_of(p * span, span), span)
        ks[dst, :] = k_ref[src, :]
        vs[dst, :] = v_ref[src, :]
        return 0

    lax.fori_loop(0, seq // span, place, 0)

    def turn(c, _):
        rows = pl.ds(pl.multiple_of(c * KEYS, KEYS), KEYS)
        kt[c] = ks[rows, :].T
        dk_acc[rows, :] = jnp.zeros((KEYS, HD), jnp.float32)
        dv_acc[rows, :] = jnp.zeros((KEYS, HD), jnp.float32)
        return 0

    lax.fori_loop(0, seq // KEYS, turn, 0)

    def one_slot(s, _):
        rows = pl.ds(pl.multiple_of(s * span, span), span)
        for g in range(GROUPS):
            part = slice(g * span, (g + 1) * span)
            cols = slice(g * HD, (g + 1) * HD)
            qs[part, :] = q_ref[rows, cols]
            ds_rows[part, :] = d_ref[rows, cols]
        qt[...] = qs[...].T
        dt[...] = ds_rows[...].T
        dqt[...] = jnp.zeros_like(dqt)
        my_span = my_span_ref[s]

        def block(c, masked, size=1):
            wide = qt.shape[1]
            cuts = [slice(j, min(j + KEYS, wide)) for j in range(0, wide, KEYS)]
            tiles = [(i, cut) for i in range(size) for cut in cuts]

            def keys_of(i):
                return pl.ds(pl.multiple_of((c + i) * KEYS, KEYS), KEYS)

            def products(i, cut):
                scores = jnp.dot(ks[keys_of(i), :], qt[:, cut], preferred_element_type=jnp.float32)
                dprob = jnp.dot(vs[keys_of(i), :], dt[:, cut], preferred_element_type=jnp.float32)
                return scores, dprob

            probs, dscores = [], []
            ahead = products(*tiles[0])
            for n, (i, cut) in enumerate(tiles):
                scores, dprob = ahead
                if n + 1 < len(tiles):
                    ahead = products(*tiles[n + 1])
                prob = jnp.exp2(scores * (inv_root * LOG2E) - lse_ref[0, s][:, cut])
                if masked:
                    key_pos = (c + i) * KEYS + lax.broadcasted_iota(jnp.int32, prob.shape, 0)
                    prob = jnp.where(my_span * span + base_ref[:, cut] >= key_pos, prob, 0.0)
                dscores.append((prob * (dprob - delta_ref[0, s][:, cut])).astype(jnp.bfloat16))
                probs.append(prob.astype(jnp.bfloat16))
                if cut is cuts[-1]:
                    prob_low = jnp.concatenate(probs[-len(cuts):], axis=1)
                    dscore = jnp.concatenate(dscores[-len(cuts):], axis=1)
                    dv_acc[keys_of(i), :] += jnp.dot(
                        prob_low, ds_rows[...], preferred_element_type=jnp.float32
                    )
                    dk_acc[keys_of(i), :] += jnp.dot(
                        dscore, qs[...], preferred_element_type=jnp.float32
                    )
                    dqt[...] += jnp.dot(kt[c + i], dscore, preferred_element_type=jnp.float32)

        whole = (my_span * span) // KEYS
        last = (my_span * span + span + KEYS - 1) // KEYS
        lax.fori_loop(0, whole // 2, lambda c, _: (block(2 * c, False, 2), 0)[1], 0)

        @pl.when(whole % 2 == 1)
        def _():
            block(whole - 1, False)

        lax.fori_loop(whole, last, lambda c, _: (block(c, True), 0)[1], 0)

        dq = (dqt[...].T * inv_root).astype(jnp.bfloat16)
        for g in range(GROUPS):
            dq_ref[rows, g * HD:(g + 1) * HD] = dq[g * span:(g + 1) * span, :]
        return 0

    lax.fori_loop(0, slots, one_slot, 0)

    def back(p, _):
        dst = pl.ds(pl.multiple_of(slot_of_ref[p] * span, span), span)
        src = pl.ds(pl.multiple_of(p * span, span), span)
        dk_ref[dst, :] = (dk_acc[src, :] * inv_root).astype(dk_ref.dtype)
        dv_ref[dst, :] = dv_acc[src, :].astype(dv_ref.dtype)
        return 0

    lax.fori_loop(0, seq // span, back, 0)


def attend(slot_of, my_spans, q, d, k, v, lse, delta, span, part_type):
    rows = q.shape[0]
    seq = k.shape[0]
    kv_heads = k.shape[1] // HD
    slots = rows // span
    wide = GROUPS * span
    base = jnp.tile(jnp.arange(span, dtype=jnp.int32), GROUPS)[None, :]
    pairs = kv_heads * wide * seq * slots

    def by_head(height, width):
        return pl.BlockSpec((height, width), lambda h, *_: (0, h))

    row_terms = pl.BlockSpec((1, slots, 1, wide), lambda h, *_: (h, 0, 0, 0))
    return pl.pallas_call(
        attend_kernel,
        grid_spec=pltpu.PrefetchScalarGridSpec(
            num_scalar_prefetch=2,
            grid=(kv_heads,),
            in_specs=[
                by_head(rows, GROUPS * HD), by_head(rows, GROUPS * HD),
                by_head(seq, HD), by_head(seq, HD),
                row_terms, row_terms,
                pl.BlockSpec((1, wide), lambda h, *_: (0, 0)),
            ],
            out_specs=[by_head(rows, GROUPS * HD), by_head(seq, HD), by_head(seq, HD)],
            scratch_shapes=[
                pltpu.VMEM((seq, HD), jnp.bfloat16),
                pltpu.VMEM((seq // KEYS, HD, KEYS), jnp.bfloat16),
                pltpu.VMEM((seq, HD), jnp.bfloat16),
                pltpu.VMEM((wide, HD), jnp.bfloat16),
                pltpu.VMEM((HD, wide), jnp.bfloat16),
                pltpu.VMEM((wide, HD), jnp.bfloat16),
                pltpu.VMEM((HD, wide), jnp.bfloat16),
                pltpu.VMEM((HD, wide), jnp.float32),
                pltpu.VMEM((seq, HD), jnp.float32),
                pltpu.VMEM((seq, HD), jnp.float32),
            ],
        ),
        out_shape=[
            jax.ShapeDtypeStruct(q.shape, jnp.bfloat16),
            jax.ShapeDtypeStruct(k.shape, part_type),
            jax.ShapeDtypeStruct(k.shape, part_type),
        ],
        compiler_params=pltpu.CompilerParams(vmem_limit_bytes=48 * 2**20),
        cost_estimate=pl.CostEstimate(
            flops=7 * pairs * HD, bytes_accessed=2**24, transcendentals=pairs // 2
        ),
        name="attend",
    )(slot_of, my_spans, q, d, k, v, lse, delta, base)


MESH = pl.DeviceIdType.MESH
NX = 2


def place_of():
    me = lax.axis_index("ctx")
    return me // (2 * NX), (me // 2) % NX, me % 2, lax.axis_index("head")


def device_at(z, x, core, y):
    return ((z * NX + x) * 2 + core, y)


def greet(nz, ny):
    z, x, core, y = place_of()
    barrier = pltpu.get_barrier_semaphore()

    def hello(device):
        pl.semaphore_signal(barrier, inc=1, device_id=device, device_id_type=MESH)

    for dy in range(ny):
        for dc in range(2):
            if dy or dc:
                hello(device_at(z, x, (core + dc) % 2, (y + dy) % ny))
    hello(device_at(z, 1 - x, core, y))

    @pl.when(z > 0)
    def _():
        hello(device_at(z - 1, x, core, y))

    @pl.when(z < nz - 1)
    def _():
        hello(device_at(z + 1, x, core, y))

    @pl.when((z == 0) | (z == nz - 1))
    def _():
        pl.semaphore_wait(barrier, 2 * ny + 1)

    @pl.when((z > 0) & (z < nz - 1))
    def _():
        pl.semaphore_wait(barrier, 2 * ny + 2)


def remote(src, dst, sems, index, device):
    return pltpu.make_async_remote_copy(
        src_ref=src, dst_ref=dst, send_sem=sems.at[(0, *index)], recv_sem=sems.at[(1, *index)],
        device_id=device, device_id_type=MESH,
    )


def aligned(index, size):
    return pl.ds(pl.multiple_of(index * size, size), size)


def spread_kernel(
    nz, ny, q_hbm, o_hbm, k_in, v_in, d_hbm, l_in, q_hbm_out, d_hbm_out, k_out, v_out, l_out, delta_out,
    q_in, o_in, d_in, q_out, o_out, d_out, local_sems,
    pair_sems, group_sems, up_sems, down_sems, side_sems,
):
    z, x, core, y = place_of()
    other = 1 - core
    own = k_in.shape[0]
    rows = 2 * own
    share = d_in.shape[0]
    sibling = device_at(z, x, other, y)
    staged = [
        pltpu.make_async_copy(src, dst, local_sems.at[n])
        for n, (src, dst) in enumerate(((d_hbm, d_in), (q_hbm, q_in), (o_hbm, o_in)))
    ]
    flushed = [
        pltpu.make_async_copy(src, dst, local_sems.at[3 + n])
        for n, (src, dst) in enumerate(((d_out, d_hbm_out), (q_out, q_hbm_out)))
    ]
    for copy in staged:
        copy.start()
    greet(nz, ny)

    chip_row = (z * NX + x) * rows
    mine = pl.ds(pl.multiple_of(chip_row + core * own, own), own)
    pairs, keeps = [], []
    for n, (src, dst, where) in enumerate((
        (k_in, k_out, mine), (v_in, v_out, mine),
        (q_in, q_out, aligned(core, own)), (o_in, o_out, aligned(core, own)),
    )):
        width = dst.shape[1]
        pairs.append(remote(
            src.at[:, aligned(other, width)], dst.at[where, :], pair_sems, (n,), sibling
        ))
        keeps.append((dst, where, src, aligned(core, width)))
    width = d_out.shape[1]
    group = []
    d_rows = aligned(core * ny + y, share)
    for dy in range(ny):
        for dc in range(2):
            yy, cc = (y + dy) % ny, (core + dc) % 2
            columns = aligned(yy * 2 + cc, width)
            if dy or dc:
                group.append(remote(
                    d_in.at[:, columns], d_out.at[d_rows, :], group_sems, (dy, dc),
                    device_at(z, x, cc, yy),
                ))
            else:
                keeps.append((d_out, d_rows, d_in, columns))
    heads = l_out.shape[1]
    pairs.append(remote(l_in.at[aligned(other, heads), :], l_out.at[core], pair_sems, (4,), sibling))

    def keep(n):
        dst, where, src, columns = keeps[n]
        dst[where, :] = src[:, columns]

    for n in range(2):
        pairs[n].start()
        keep(n)
    for n in range(2):
        pairs[n].wait_recv()

    def hop(n, zz, sems, device):
        ref = (k_out, v_out)[n].at[aligned(zz * NX + x, rows), :]
        return remote(ref, ref, sems, (n, zz), device)

    def up(n, zz):
        return hop(n, zz, up_sems, device_at(z + 1, x, core, y))

    def down(n, zz):
        return hop(n, zz, down_sems, device_at(z - 1, x, core, y))

    def side(n, zz):
        return hop(n, zz, side_sems, device_at(z, 1 - x, core, y))

    def side_in(n, zz):
        ref = (k_out, v_out)[n].at[aligned(zz * NX + 1 - x, rows), :]
        return remote(ref, ref, side_sems, (n, zz), device_at(z, 1 - x, core, y))

    for n in range(2):
        @pl.when(z < nz - 1)
        def _():
            up(n, z).start()

        @pl.when(z > 0)
        def _():
            down(n, z).start()

        side(n, z).start()
    staged[0].wait()
    for copy in reversed(group):
        copy.start()
    staged[1].wait()
    staged[2].wait()
    for n in range(2, 5):
        pairs[n].start()
        keep(n)
    l_out[core] = l_in[aligned(core, heads), :]

    for step in range(1, nz):
        for n in range(2):
            @pl.when(z - step >= 0)
            def _():
                up(n, z - step).wait_recv()

                @pl.when(z < nz - 1)
                def _():
                    up(n, z - step).start()

                side(n, z - step).start()

            @pl.when(z + step < nz)
            def _():
                down(n, z + step).wait_recv()

                @pl.when(z > 0)
                def _():
                    down(n, z + step).start()

                side(n, z + step).start()

    for copy in group + pairs[2:]:
        copy.wait()
    for copy in flushed:
        copy.start()
    for h in range(delta_out.shape[0]):
        cols = slice(h * HD, (h + 1) * HD)
        terms = d_out[:, cols].astype(jnp.float32) * o_out[:, cols].astype(jnp.float32)
        delta_out[h:h + 1, :] = jnp.sum(terms.T, axis=0, keepdims=True)

    for n in range(2):
        for zz in range(nz):
            side_in(n, zz).wait_recv()
            side(n, zz).wait_send()

            @pl.when((zz <= z) & (z < nz - 1))
            def _():
                up(n, zz).wait_send()

            @pl.when((zz >= z) & (z > 0))
            def _():
                down(n, zz).wait_send()

        pairs[n].wait_send()
    for copy in flushed:
        copy.wait()


def spread(q, o, k, v, d, lse, ctx, ny):
    nz = ctx // (2 * NX)
    rows = 2 * q.shape[0]
    seq = k.shape[0] * ctx

    def like(height, x, parts):
        return jax.ShapeDtypeStruct((height, x.shape[1] // parts), x.dtype)

    anywhere = pl.BlockSpec(memory_space=pltpu.HBM)
    whole = pl.BlockSpec(memory_space=pltpu.VMEM)
    dma = pltpu.SemaphoreType.DMA
    return pl.pallas_call(
        functools.partial(spread_kernel, nz, ny),
        out_shape=[like(rows, q, 2), like(rows, d, 2 * ny), like(seq, k, 2), like(seq, v, 2),
                   jax.ShapeDtypeStruct((2, lse.shape[0] // 2, lse.shape[1]), lse.dtype),
                   jax.ShapeDtypeStruct((lse.shape[0] // 2, rows), jnp.float32)],
        in_specs=[anywhere, anywhere, whole, whole, anywhere, whole],
        out_specs=[anywhere, anywhere, whole, whole, whole, whole],
        scratch_shapes=[
            pltpu.VMEM(q.shape, q.dtype), pltpu.VMEM(o.shape, o.dtype), pltpu.VMEM(d.shape, d.dtype),
            pltpu.VMEM((rows, q.shape[1] // 2), q.dtype), pltpu.VMEM((rows, q.shape[1] // 2), o.dtype),
            pltpu.VMEM((rows, q.shape[1] // 2), d.dtype), dma((5,)),
            dma((2, 5)), dma((2, ny, 2)), dma((2, 2, nz)), dma((2, 2, nz)), dma((2, 2, nz)),
        ],
        compiler_params=pltpu.CompilerParams(
            collective_id=0, has_side_effects=True, vmem_limit_bytes=56 * 2**20
        ),
        name="spread",
    )(q, o, k, v, d, lse)


def fold_kernel(
    nz, ny, dk_in, dv_in, dq_in, gk_out, gv_out, gq_out,
    side_buf, up_buf, down_buf, out_buf, fin,
    local_sems, pair_sems, group_sems, up_sems, down_sems, side_sems,
):
    z, x, core, y = place_of()
    other = 1 - core
    rows = fin.shape[1]
    own = rows // 2
    share = gq_out.shape[0]
    parts = (dk_in, dv_in)
    greet(nz, ny)

    def side(n, zz):
        return remote(
            parts[n].at[aligned(zz * NX + 1 - x, rows), :], side_buf.at[n, zz], side_sems, (n, zz),
            device_at(z, 1 - x, core, y),
        )

    def up(n, zz):
        return remote(
            out_buf.at[n, zz], up_buf.at[n, zz], up_sems, (n, zz), device_at(z + 1, x, core, y)
        )

    def down(n, zz):
        return remote(
            out_buf.at[n, zz], down_buf.at[n, zz], down_sems, (n, zz), device_at(z - 1, x, core, y)
        )

    order = []
    for far in range(nz // 2):
        order.append(jnp.where(z < nz // 2, nz - 1 - far, far))
        order.append(jnp.where(z < nz // 2, far, nz - 1 - far))

    width = dq_in.shape[1]
    group = []
    for dy in range(ny):
        for dc in range(2):
            yy, cc = (y + dy) % ny, (core + dc) % 2
            src = dq_in.at[aligned(cc * ny + yy, share), :]
            dst = gq_out.at[:, aligned(y * 2 + core, width)]
            if dy or dc:
                group.append(remote(src, dst, group_sems, (dy, dc), device_at(z, x, cc, yy)))
            else:
                keep = pltpu.make_async_copy(src, dst, local_sems.at[2])
    for zz in order:
        for n in range(2):
            side(n, zz).start()
    for copy in reversed(group):
        copy.start()
    keep.start()

    def total(n, zz):
        mine = parts[n][aligned(zz * NX + x, rows), :].astype(jnp.float32)
        return mine + side_buf[n, zz].astype(jnp.float32)

    for zz in order:
        for n in range(2):
            @pl.when(zz > z)
            def _():
                side(n, zz).wait_recv()

                @pl.when(z == 0)
                def _():
                    out_buf[n, zz] = total(n, zz).astype(jnp.bfloat16)

                @pl.when(z > 0)
                def _():
                    up(n, zz).wait_recv()
                    out_buf[n, zz] = (
                        total(n, zz) + up_buf[n, zz].astype(jnp.float32)
                    ).astype(jnp.bfloat16)

                up(n, zz).start()

            @pl.when(zz < z)
            def _():
                side(n, zz).wait_recv()

                @pl.when(z == nz - 1)
                def _():
                    out_buf[n, zz] = total(n, zz).astype(jnp.bfloat16)

                @pl.when(z < nz - 1)
                def _():
                    down(n, zz).wait_recv()
                    out_buf[n, zz] = (
                        total(n, zz) + down_buf[n, zz].astype(jnp.float32)
                    ).astype(jnp.bfloat16)

                down(n, zz).start()

    ends = []
    for n, out in enumerate((gk_out, gv_out)):
        side(n, z).wait_recv()

        @pl.when(z == 0)
        def _():
            down(n, z).wait_recv()
            fin[n] = (total(n, z) + down_buf[n, z].astype(jnp.float32)).astype(jnp.bfloat16)

        @pl.when(z == nz - 1)
        def _():
            up(n, z).wait_recv()
            fin[n] = (total(n, z) + up_buf[n, z].astype(jnp.float32)).astype(jnp.bfloat16)

        @pl.when((z > 0) & (z < nz - 1))
        def _():
            up(n, z).wait_recv()
            down(n, z).wait_recv()
            fin[n] = (
                total(n, z) + up_buf[n, z].astype(jnp.float32) + down_buf[n, z].astype(jnp.float32)
            ).astype(jnp.bfloat16)

        columns = aligned(core, fin.shape[2])
        pair = remote(
            fin.at[n, aligned(other, own), :], out.at[:, columns], pair_sems, (n,),
            device_at(z, x, other, y),
        )
        here = pltpu.make_async_copy(
            fin.at[n, aligned(core, own), :], out.at[:, columns], local_sems.at[n]
        )
        pair.start()
        here.start()
        ends += [pair, here]

    for copy in ends + group + [keep]:
        copy.wait()
    for n in range(2):
        for zz in range(nz):
            side(n, zz).wait_send()

            @pl.when(zz > z)
            def _():
                up(n, zz).wait_send()

            @pl.when(zz < z)
            def _():
                down(n, zz).wait_send()


def fold(dk, dv, dq, ctx, ny):
    nz = ctx // (2 * NX)
    rows = dq.shape[0]
    own = rows // 2
    width = dk.shape[1]
    anywhere = pl.BlockSpec(memory_space=pl.ANY)
    whole = pl.BlockSpec(memory_space=pltpu.VMEM)
    dma = pltpu.SemaphoreType.DMA
    buffers = pltpu.VMEM((2, nz, rows, width), jnp.bfloat16)
    kv_out = jax.ShapeDtypeStruct((own, 2 * width), jnp.bfloat16)
    return pl.pallas_call(
        functools.partial(fold_kernel, nz, ny),
        out_shape=[kv_out, kv_out,
                   jax.ShapeDtypeStruct((rows // (2 * ny), dq.shape[1] * 2 * ny), jnp.bfloat16)],
        in_specs=[whole, whole, anywhere],
        out_specs=[anywhere] * 3,
        scratch_shapes=[
            buffers, buffers, buffers, buffers, pltpu.VMEM((2, rows, width), jnp.bfloat16),
            dma((3,)), dma((2, 2)), dma((2, ny, 2)), dma((2, 2, nz)), dma((2, 2, nz)), dma((2, 2, nz)),
        ],
        compiler_params=pltpu.CompilerParams(
            collective_id=1, has_side_effects=True, vmem_limit_bytes=32 * 2**20
        ),
        name="fold",
    )(dk, dv, dq)


def row_terms_of(terms, kv_heads, span):
    rows = terms.shape[1]
    cut = terms.reshape(kv_heads, GROUPS, rows // span, span)
    return cut.transpose(0, 2, 1, 3).reshape(kv_heads, rows // span, 1, GROUPS * span)


def per_device(query_rows, key_rows, value_rows, attn_output, log_norms, grad_output, span_order):
    own_rows = query_rows.shape[0]
    span = own_rows // 2
    ctx = lax.axis_size("ctx")
    me = lax.axis_index("ctx")
    cores = 2 if (key_rows.shape[1] // HD) % 2 == 0 and ctx % 2 == 0 else 1
    chip_groups = [[i * cores + c for c in range(cores)] for i in range(ctx // cores)]
    ring_groups = [[i * cores + c for i in range(ctx // cores)] for c in range(cores)]

    def to_heads(x, split=1, concat=0):
        if cores == 1:
            return x
        return lax.all_to_all(
            x, "ctx", split_axis=split, concat_axis=concat, axis_index_groups=chip_groups, tiled=True
        )

    ny = lax.axis_size("head")
    by_kernels = cores == 2 and ctx % (4 * NX) == 0
    if by_kernels:
        q, d, k, v, lse, delta = spread(
            query_rows, attn_output, key_rows, value_rows, grad_output, log_norms, ctx, ny
        )
        lse = jnp.concatenate([lse[0], lse[1]], axis=1)
    else:
        lse = to_heads(log_norms, 0, 1)
        q = to_heads(query_rows)
        o = to_heads(attn_output)
        d = to_heads(lax.all_to_all(grad_output, "head", split_axis=1, concat_axis=0, tiled=True))
        kv = jnp.concatenate([to_heads(key_rows), to_heads(value_rows)], axis=1)
        kv = lax.all_gather(kv, "ctx", axis=0, axis_index_groups=ring_groups, tiled=True)
        k, v = kv[:, :kv.shape[1] // 2], kv[:, kv.shape[1] // 2:]
    half = k.shape[1]
    kv_heads = half // HD
    rows = q.shape[0]
    if not by_kernels:
        terms = d.astype(jnp.float32) * o.astype(jnp.float32)
        delta = jnp.sum(terms.reshape(rows, kv_heads * GROUPS, HD), axis=-1).T
    spans = span_order.shape[0]
    slots = rows // span
    ids = jnp.arange(spans, dtype=jnp.int32)
    slot_of = jnp.sum(jnp.where(span_order[None, :] == ids[:, None], ids[None, :], 0), axis=1)
    my_spans = lax.dynamic_slice_in_dim(span_order, (me // cores) * slots, slots)
    dq, dk, dv = attend(
        slot_of, my_spans, q, d, k, v,
        row_terms_of(lse * LOG2E, kv_heads, span), row_terms_of(delta, kv_heads, span),
        span, jnp.bfloat16 if by_kernels else jnp.float32,
    )
    if by_kernels:
        grad_key, grad_value, grad_query = fold(dk, dv, dq, ctx, ny)
        return (grad_query, grad_key, grad_value)
    dkv = jnp.concatenate([dk, dv], axis=1)
    dkv = lax.psum_scatter(dkv, "ctx", scatter_dimension=0, axis_index_groups=ring_groups, tiled=True)
    dkv = dkv.astype(jnp.bfloat16)
    grad_key = to_heads(dkv[:, :half], 0, 1)
    grad_value = to_heads(dkv[:, half:], 0, 1)
    dq = to_heads(dq, 0, 1)
    grad_query = lax.all_to_all(dq, "head", split_axis=0, concat_axis=1, tiled=True)
    return (grad_query, grad_key, grad_value)


def solution(mesh):
    return jax.shard_map(
        per_device,
        mesh=mesh,
        in_specs=(
            P("ctx", "head"),
            P("ctx", "head"),
            P("ctx", "head"),
            P("ctx", "head"),
            P("head", "ctx"),
            P(("ctx", "head"), None),
            P(),
        ),
        out_specs=(P(("ctx", "head"), None), P("ctx", "head"), P("ctx", "head")),
        check_vma=False,
    )
```
